32 devices in a mesh: groups: 2 (over y), dp: 8 (over z, x), mp: 2 (over core).
Axes of the slice: x: 2, y: 2, z: 4, core: 2. Of those that a mesh axis runs over, the one named last changes fastest.
Arguments:
- hidden_input: bfloat16 [2048, 8192], P(('groups', 'dp')), parts along dimension 0, may hold values from -6 to 6
- upstream: bfloat16 [2048, 1024], P(('groups', 'dp')), parts along dimension 0, may hold values from -6 to 6
- rollout_row_counts: int32 [2048], P(('groups', 'dp')), parts along dimension 0, may hold values from 0 to 4
- tenant_of_block: int32 [16], P('groups'), parts along dimension 0, may hold values from 0 to 15
- frozen_value_weight: bfloat16 [8192, 1024], P('mp', 'dp'), may hold values from -0.1875 to 0.1875
- common_down_factor: bfloat16 [8192, 64], replicated, may hold values from -0.0625 to 0.0625
- adapter_up_factor: bfloat16 [32, 64, 1024], P(('groups', 'dp')), parts along dimension 0, may hold values from -0.75 to 0.75
Outputs:
- input_gradient: bfloat16 [2048, 8192], P(('groups', 'dp'), 'mp'), parts along dimension 0
- up_factor_gradient: bfloat16 [32, 64, 1024], P(('groups', 'dp')), parts along dimension 0
The draws below stay inside these ranges and needn't reach their ends.
There are 2 independent parts, one for each index of `groups`. The reference program is written for one: setup_inputs(seed, part) draws one part's arguments, and reference() takes and returns one part's arrays. A program takes and returns all parts, laid end to end along the dimension named above; an argument that names none is the same for every part. Nothing has to cross between parts.
All inputs are finite; a program needn't handle non-finite values.
Results may differ from the reference program's by a relative error of at most 0.0054.
Values may be sent and summed in bfloat16 or wider, within the bound.
No kernel may reach another device: no remote copies, remote signals or barrier semaphores. Data moves between devices by JAX's collectives and lax.ppermute only.
A program may use at most 64 MiB of HBM per device.

```python
import math
import jax
import jax.numpy as jnp
import numpy as np
from jax import lax

D = 8192
VALUE_WIDTH = 1024
ADAPTER_RANK = 64
TENANT_BLOCK = 128
TENANT_COUNT = 16
NBLK = 8
ROWS = 1024


def plant(drawn, key, low, high):
    longest = drawn.shape.index(max(drawn.shape))
    spots = []
    for shift in (0, 1):
        where = [jax.random.randint(jax.random.fold_in(key, axis), (), 0, length) for axis, length in enumerate(drawn.shape)]
        where[longest] = (where[longest] + shift) % drawn.shape[longest]
        spots.append(tuple(where))
    return drawn.at[spots[0]].set(low).at[spots[1]].set(high)


def steps_of(own_key, dims, split, least, top_value):
    gain = 1.0
    for axis_at, blocks in split:
        steps = jax.random.uniform(jax.random.fold_in(jax.random.fold_in(own_key, 6), axis_at), (blocks,), jnp.float32, least / len(split), top_value / len(split))
        gain = gain * jnp.repeat(jnp.exp(steps), dims[axis_at] // blocks).reshape((-1,) + (1,) * (len(dims) - 1 - axis_at))
    return gain


def cumulative_ranks(amount, skew):
    portions = [(1 << 20) // math.isqrt(standing ** skew) + 1 for standing in range(1, amount + 1)]
    spread = 1 + sum(portions) // (1 << 30)
    return np.cumsum(np.array([max(1, weight // spread) for weight in portions]))


def ranked(stream_key, shape, amount, lean):
    grid = cumulative_ranks(amount, lean)
    lot = jax.random.randint(jax.random.fold_in(stream_key, 1), shape, 0, int(grid[amount - 1]))
    grade = jnp.searchsorted(jnp.asarray(grid, jnp.int32), lot, side="right")
    return jax.random.permutation(jax.random.fold_in(stream_key, 2), amount)[grade].astype(jnp.int32)


def scatter_about(stream_key, shape, spread, bound, shards=(), kind=jnp.bfloat16):
    drawn = spread * jax.random.normal(stream_key, shape, jnp.float32)
    if shards:
        drawn = drawn * steps_of(stream_key, shape, shards, -0.22, 0.18)
    return jnp.clip(drawn, -bound, bound).astype(kind)


def setup_inputs(seed: int = 0, part: int = 0) -> dict:
    arg_keys = jax.random.split(jax.random.key(seed), 8)
    own_keys = jax.random.split(jax.random.fold_in(arg_keys[7], part), 8)
    hidden_input = scatter_about(own_keys[0], (ROWS, D), 1.0, 6.0, ((0, 8),))
    upstream = scatter_about(own_keys[1], (ROWS, VALUE_WIDTH), 1.0, 6.0, ((0, 8),))
    rollout_row_counts = plant(jax.random.randint(own_keys[2], (ROWS,), 0, 5), jax.random.fold_in(own_keys[2], 1), 0, 4).astype(jnp.int32)
    tenant_of_block = plant(ranked(own_keys[3], (NBLK,), TENANT_COUNT, 2), jax.random.fold_in(own_keys[3], 3), 0, TENANT_COUNT - 1).astype(jnp.int32)
    frozen_value_weight = scatter_about(arg_keys[4], (D, VALUE_WIDTH), VALUE_WIDTH ** -0.5, 0.1875, ((0, 2), (1, 8)))
    common_down_factor = scatter_about(arg_keys[5], (D, ADAPTER_RANK), D ** -0.5, 0.0625)
    adapter_up_factor = scatter_about(own_keys[6], (TENANT_COUNT, ADAPTER_RANK, VALUE_WIDTH), ADAPTER_RANK ** -0.5, 0.75, ((0, 8),))
    return dict(hidden_input=hidden_input, upstream=upstream, rollout_row_counts=rollout_row_counts, tenant_of_block=tenant_of_block, frozen_value_weight=frozen_value_weight, common_down_factor=common_down_factor, adapter_up_factor=adapter_up_factor)


adapter_scale = 2.0


def reference(hidden_input, upstream, rollout_row_counts, tenant_of_block, frozen_value_weight, common_down_factor, adapter_up_factor):
    weighted = (rollout_row_counts[:, None].astype(jnp.float32) * upstream.astype(jnp.float32)).astype(jnp.bfloat16)
    low_rank = jnp.dot(hidden_input, common_down_factor, preferred_element_type=jnp.float32).astype(jnp.bfloat16)
    selected = adapter_up_factor[tenant_of_block.astype(jnp.int32)]
    grad_blocks = weighted.reshape(NBLK, TENANT_BLOCK, VALUE_WIDTH).astype(jnp.float32)
    backward_rank = jnp.einsum("brc,bkc->brk", grad_blocks, selected.astype(jnp.float32))
    backward_rank = backward_rank.reshape(ROWS, ADAPTER_RANK).astype(jnp.bfloat16)
    frozen_term = jnp.dot(weighted, frozen_value_weight.T, preferred_element_type=jnp.float32)
    adapter_term = jnp.dot(backward_rank, common_down_factor.T, preferred_element_type=jnp.float32)
    input_gradient = (frozen_term + adapter_scale * adapter_term).astype(jnp.bfloat16)
    code_blocks = low_rank.reshape(NBLK, TENANT_BLOCK, ADAPTER_RANK).astype(jnp.float32)
    per_block = jnp.einsum("brk,brc->bkc", code_blocks, grad_blocks)
    onehot = (tenant_of_block[None, :] == jnp.arange(TENANT_COUNT, dtype=jnp.int32)[:, None]).astype(jnp.float32)
    reduced_total = jnp.einsum("tb,bkc->tkc", onehot, per_block, precision=lax.Precision.HIGHEST)
    up_factor_gradient = (reduced_total * (adapter_scale / TENANT_BLOCK)).astype(jnp.bfloat16)
    return input_gradient, up_factor_gradient
```

```python
import math

import jax
import jax.numpy as jnp
from jax import lax
from jax.sharding import PartitionSpec as P

adapter_scale = 2.0
ALL = ("groups", "dp", "mp")


def local(
    hidden_input,
    upstream,
    rollout_row_counts,
    tenant_of_block,
    frozen_value_weight,
    common_down_factor,
    adapter_up_factor,
):
    f32, bf16 = jnp.float32, jnp.bfloat16
    group_count = lax.axis_size("groups")
    dp_count = lax.axis_size("dp")
    mp_count = lax.axis_size("mp")
    g = lax.axis_index("groups")
    m = lax.axis_index("mp")
    half_width, cols = frozen_value_weight.shape
    tenants_here, rank, out_width = adapter_up_factor.shape
    part_rank = rank // mp_count
    rows = hidden_input.shape[0]
    blocks = tenant_of_block.shape[0]
    block_rows = rows * dp_count // blocks
    tenants = tenants_here * dp_count

    near = math.gcd(4, dp_count)
    team = group_count * near
    features = half_width // team
    teams = [
        [(gi * dp_count + base + k) * mp_count + mi for gi in range(group_count) for k in range(near)]
        for base in range(0, dp_count, near)
        for mi in range(mp_count)
    ]

    weighted = (rollout_row_counts[:, None].astype(f32) * upstream.astype(f32)).astype(bf16)

    group_weight = lax.dynamic_slice_in_dim(frozen_value_weight, g * near * features, near * features, 0)
    to_send = jnp.broadcast_to(
        group_weight.reshape(1, near, features, cols), (dp_count // near, near, features, cols)
    ).reshape(dp_count, features, cols)
    weight_slices = lax.all_to_all(to_send, "dp", split_axis=0, concat_axis=0, tiled=True)

    part_cols = out_width // mp_count
    my_cols = lax.dynamic_slice_in_dim(weighted, m * part_cols, part_cols, 1)
    row_parts = lax.all_to_all(
        jnp.broadcast_to(my_cols[None], (team, rows, part_cols)),
        ALL, split_axis=0, concat_axis=0, tiled=True, axis_index_groups=teams,
    )
    other_parts = lax.ppermute(row_parts, "mp", [(k, (k + 1) % mp_count) for k in range(mp_count)])

    down_part = lax.dynamic_slice_in_dim(common_down_factor, m * part_rank, part_rank, 1)
    low = lax.dot_general(
        down_part, hidden_input, (((0,), (1,)), ((), ())), preferred_element_type=f32
    ).astype(bf16)
    up_part = lax.dynamic_slice_in_dim(adapter_up_factor, m * part_rank, part_rank, 1)
    weighted_send = weighted.reshape(rows, dp_count, cols).transpose(1, 0, 2)
    up_send = up_part.reshape(tenants_here * part_rank, dp_count, cols).transpose(1, 0, 2)
    low_send = jnp.broadcast_to(low.reshape(1, -1, cols), (dp_count, part_rank * rows // cols, cols))
    first = lax.all_to_all(
        jnp.concatenate([weighted_send, up_send, low_send], axis=1),
        "dp", split_axis=0, concat_axis=0, tiled=True,
    )
    at_up, at_low = rows, rows + tenants_here * part_rank
    grad_blocks = first[:, :at_up].reshape(blocks, block_rows, cols)
    up_cols = first[:, at_up:at_low].reshape(tenants, part_rank, cols)
    low_blocks = (
        first[:, at_low:].reshape(dp_count, part_rank, blocks // dp_count, block_rows)
        .transpose(0, 2, 1, 3).reshape(blocks, part_rank, block_rows)
    )
    selected = up_cols[tenant_of_block]
    term = jnp.einsum("bkc,brc->bkr", selected, grad_blocks, preferred_element_type=f32)
    per_block = jnp.einsum("bkr,brc->bkc", low_blocks, grad_blocks, preferred_element_type=f32)
    onehot = (tenant_of_block[None, :] == jnp.arange(tenants, dtype=jnp.int32)[:, None]).astype(f32)
    tenant_sums = jnp.einsum("tb,bkc->tkc", onehot, per_block, precision=lax.Precision.HIGHEST)
    finished = (tenant_sums * (adapter_scale / block_rows)).astype(bf16)
    term_send = (
        term.astype(bf16).reshape(dp_count, blocks // dp_count, part_rank, block_rows)
        .transpose(0, 2, 1, 3).reshape(dp_count, part_rank * rows // cols, cols)
    )
    second = lax.all_to_all(
        jnp.concatenate([term_send, finished.reshape(dp_count, tenants_here * part_rank, cols)], axis=1),
        "dp", split_axis=0, concat_axis=0, tiled=True,
    )
    at_grad = term_send.shape[1]
    back_part = jnp.sum(second[:, :at_grad].astype(f32), axis=0).astype(bf16).reshape(part_rank, rows)
    grad_part = (
        second[:, at_grad:].reshape(dp_count, tenants_here, part_rank, cols)
        .transpose(1, 2, 0, 3).reshape(tenants_here, part_rank, out_width)
    )
    back_rank = lax.all_gather(back_part, "mp", axis=0, tiled=True)
    up_factor_gradient = lax.all_gather(grad_part, "mp", axis=1, tiled=True)

    def partial_term(parts, which):
        slices = lax.dynamic_slice_in_dim(weight_slices, which * (dp_count // mp_count), dp_count // mp_count, 0)
        return lax.dot_general(
            parts.reshape(team * rows, part_cols),
            slices.transpose(1, 0, 2).reshape(features, part_cols),
            (((1,), (1,)), ((), ())),
            preferred_element_type=f32,
        )

    frozen = (partial_term(row_parts, m) + partial_term(other_parts, (m + mp_count - 1) % mp_count)).astype(bf16)
    frozen_mine = lax.all_to_all(
        frozen.reshape(team, rows, features),
        ALL, split_axis=0, concat_axis=0, tiled=True, axis_index_groups=teams,
    )
    frozen_term = frozen_mine.transpose(1, 0, 2).reshape(rows, half_width)
    down_half = lax.dynamic_slice_in_dim(common_down_factor, m * half_width, half_width, 0)
    adapter_term = lax.dot_general(
        back_rank, down_half, (((0,), (1,)), ((), ())), preferred_element_type=f32
    )
    input_gradient = (frozen_term.astype(f32) + adapter_scale * adapter_term).astype(bf16)
    return (input_gradient, up_factor_gradient)


def solution(mesh):
    placed = (
        P(("groups", "dp"), None),
        P(("groups", "dp"), None),
        P(("groups", "dp")),
        P("groups"),
        P("mp", "dp"),
        P(),
        P(("groups", "dp"), None, None),
    )
    return jax.shard_map(
        local,
        mesh=mesh,
        in_specs=placed,
        out_specs=(P(("groups", "dp"), "mp"), P(("groups", "dp"), None, None)),
        check_vma=False,
    )
```

```python
import functools
import math

import jax
import jax.numpy as jnp
from jax import lax
from jax.experimental import pallas as pl
from jax.experimental.pallas import tpu as pltpu
from jax.sharding import PartitionSpec as P

adapter_scale = 2.0
ALL = ("groups", "dp", "mp")
f32, bf16 = jnp.float32, jnp.bfloat16
VMEM = pl.BlockSpec(memory_space=pltpu.VMEM)
SMEM = pl.BlockSpec(memory_space=pltpu.SMEM)
HBM = pl.BlockSpec(memory_space=pltpu.HBM)
PARAMS = pltpu.CompilerParams(vmem_limit_bytes=16 * 1024 * 1024)


def place():
    return lax.axis_index("groups"), lax.axis_index("dp"), lax.axis_index("mp")


def piece(index, size):
    return pl.ds(pl.multiple_of(index * size, size), size)


def prepare_kernel(
    leaving, weight, upstream, counts, tenants, up, to_send, weighted, my_cols, picked,
    held_weight, held_upstream, held_counts, held_tenants, held_up, in_sem, out_sem, other_sem,
):
    g, _, m = place()
    copies, depth = to_send.shape[0], to_send.shape[1]
    chunks = in_sem.shape[0]
    size = depth // chunks
    others = [
        pltpu.make_async_copy(source, target, other_sem.at[i])
        for i, (source, target) in enumerate(
            [(counts, held_counts), (upstream, held_upstream), (tenants, held_tenants), (up, held_up)]
        )
    ]
    for load in others:
        load.start()
    loads, stores = [], []
    for c in range(chunks):
        at = pl.ds(pl.multiple_of(g * depth + c * size, size), size)
        loads.append(pltpu.make_async_copy(weight.at[at], held_weight.at[pl.ds(c * size, size)], in_sem.at[c]))
        loads[-1].start()
    rows, part = my_cols.shape
    diagonal = lax.broadcasted_iota(jnp.int32, (rows, rows), 0) == lax.broadcasted_iota(jnp.int32, (rows, rows), 1)
    others[0].wait()
    scale = jnp.where(diagonal, held_counts[...].astype(f32), 0.0).astype(bf16)
    others[1].wait()
    weighted[...] = jnp.dot(scale, held_upstream[...], preferred_element_type=f32).astype(bf16)
    my_cols[...] = weighted[:, piece(m, part)]
    for c in range(chunks):
        loads[c].wait()
        for k in range(copies):
            at = pl.ds(c * size, size)
            stores.append(pltpu.make_async_copy(held_weight.at[at], to_send.at[k, at], out_sem.at[k, c]))
            stores[-1].start()
    others[2].wait()
    others[3].wait()
    for i, k in enumerate(leaving):
        for n in range(picked.shape[1]):
            picked[i, n] = chosen(held_tenants, held_up, k, n, picked.shape[1], picked.shape[2])
    for store in stores:
        store.wait()


def chosen(tenants, up, distance, n, own_blocks, part_rank):
    _, d, m = place()
    wanted = tenants[(d ^ distance) * own_blocks + n] - d * up.shape[0]
    total = jnp.zeros((part_rank, up.shape[2]), bf16)
    for t in range(up.shape[0]):
        total = jnp.where(wanted == t, up[t, piece(m, part_rank)], total)
    return total


def pick_kernel(leaving, held, tenants, up, *refs):
    out = refs[-1]
    for i, k in enumerate(leaving):
        for n in range(out.shape[1]):
            value = chosen(tenants, up, k, n, out.shape[1], out.shape[2])
            for kept, got in zip(held, refs[:-1]):
                value = value + got[kept.index(k), n]
            out[i, n] = value


def back_kernel(held, tenants, up, weighted, *refs):
    out = refs[-1]
    part_rank, rows = out.shape
    own_blocks = refs[0].shape[1]
    size = rows // own_blocks
    for n in range(own_blocks):
        value = chosen(tenants, up, 0, n, own_blocks, part_rank)
        for kept, got in zip(held, refs[:-1]):
            value = value + got[kept.index(0), n]
        at = slice(n * size, (n + 1) * size)
        out[:, at] = lax.dot_general(
            value, weighted[at], (((1,), (1,)), ((), ())), preferred_element_type=f32
        ).astype(bf16)


def block_kernel(down, hidden, weighted, out):
    _, own_blocks, part_rank, _ = out.shape
    size = weighted.shape[0] // own_blocks
    _, _, m = place()
    low = lax.dot_general(
        down[piece(m, part_rank)], hidden[...], (((1,), (1,)), ((), ())), preferred_element_type=f32
    ).astype(bf16)
    for n in range(own_blocks):
        at = slice(n * size, (n + 1) * size)
        out[0, n] = jnp.dot(low[:, at], weighted[at], preferred_element_type=f32).astype(bf16)


def gradient_kernel(orders, scale, tenants, *refs):
    out = refs[-1]
    _, d, _ = place()
    for t in range(out.shape[0]):
        total = jnp.zeros(out.shape[1:], f32)
        for order, got in zip(orders, refs[:-1]):
            own_blocks = got.shape[1]
            for i, k in enumerate(order):
                for n in range(own_blocks):
                    wanted = tenants[(d ^ k) * own_blocks + n] - d * out.shape[0]
                    total = total + jnp.where(wanted == t, got[i, n].astype(f32), 0.0)
        out[t] = (total * scale).astype(bf16)


def frozen_kernel(near, distances, mine, other, slices, out, held):
    team, rows, part = mine.shape
    count, features, width = slices.shape
    per_part = count // 2
    g, d, m = place()
    own = g * near + lax.rem(d, near)
    for half in range(2):
        at = lax.rem(m + half, 2) * per_part
        for j in range(per_part):
            held[half, :, j * width : (j + 1) * width] = slices[at + j]
    dims = (((1,), (1,)), ((), ()))
    for k, distance in enumerate(distances):
        total = lax.dot_general(mine[k], held[0], dims, preferred_element_type=f32)
        total += lax.dot_general(other[k], held[1], dims, preferred_element_type=f32)
        out[own ^ distance] = total.astype(bf16)


def last_kernel(frozen, back, down, out, held, sem):
    team, rows, features = frozen.shape
    _, _, m = place()
    stores = []
    for k in range(team):
        at = pl.ds(pl.multiple_of(m * (team * features) + k * features, features), features)
        adapter = lax.dot_general(back[...], down[:, at], (((0,), (0,)), ((), ())), preferred_element_type=f32)
        held[k] = (frozen[k].astype(f32) + adapter_scale * adapter).astype(bf16)
        stores.append(pltpu.make_async_copy(held.at[k], out.at[:, pl.ds(k * features, features)], sem.at[k]))
        stores[-1].start()
    for store in stores:
        store.wait()


def local(
    hidden_input,
    upstream,
    rollout_row_counts,
    tenant_of_block,
    frozen_value_weight,
    common_down_factor,
    adapter_up_factor,
):
    group_count = lax.axis_size("groups")
    dp_count = lax.axis_size("dp")
    mp_count = lax.axis_size("mp")
    half_width, cols = frozen_value_weight.shape
    tenants_here, rank, out_width = adapter_up_factor.shape
    part_rank = rank // mp_count
    part_cols = out_width // mp_count
    rows = hidden_input.shape[0]
    own_blocks = tenant_of_block.shape[0] // dp_count
    block_rows = rows // own_blocks

    near = math.gcd(4, dp_count)
    team = group_count * near
    features = half_width // team
    teams = [
        [(gi * dp_count + base + k) * mp_count + mi for gi in range(group_count) for k in range(near)]
        for base in range(0, dp_count, near)
        for mi in range(mp_count)
    ]

    def swap(value, axis, bit):
        size = lax.axis_size(axis)
        return lax.ppermute(value, axis, [(k, k ^ bit) for k in range(size)])

    def shape(*dims):
        return jax.ShapeDtypeStruct(dims, bf16)

    def call(kernel, name, outs, in_specs, *values, scratch=(), out_specs=VMEM, params=PARAMS):
        return pl.pallas_call(
            kernel, in_specs=in_specs, out_specs=out_specs, out_shape=outs, scratch_shapes=list(scratch),
            compiler_params=params, name=name,
        )(*values)

    dp_bits = [1 << k for k in range(dp_count.bit_length() - 1)]
    near_bits = [bit for bit in dp_bits if bit < near]
    tie = lax.optimization_barrier

    repeats = dp_count // near
    leaving = [k for k in range(dp_count) if k & 1]
    remaining = [k for k in range(dp_count) if not k & 1]
    to_send, weighted, my_cols, picked = call(
        functools.partial(prepare_kernel, leaving), "prepare",
        [
            shape(repeats, near * features, cols),
            shape(rows, out_width),
            shape(rows, part_cols),
            shape(len(leaving), own_blocks, part_rank, out_width),
        ],
        [HBM] * 5,
        frozen_value_weight, upstream, rollout_row_counts[None], tenant_of_block, adapter_up_factor,
        out_specs=[HBM, VMEM, VMEM, VMEM],
        params=pltpu.CompilerParams(),
        scratch=[
            pltpu.VMEM((near * features, cols), bf16),
            pltpu.VMEM((rows, out_width), bf16),
            pltpu.VMEM((1, rows), jnp.int32),
            pltpu.SMEM(tenant_of_block.shape, jnp.int32),
            pltpu.VMEM(adapter_up_factor.shape, bf16),
            pltpu.SemaphoreType.DMA((4,)),
            pltpu.SemaphoreType.DMA((repeats, 4)),
            pltpu.SemaphoreType.DMA((4,)),
        ],
    )
    row_steps = [("dp", bit, bit) for bit in near_bits[1:] + near_bits[:1]] + [
        ("groups", 1 << k, near << k) for k in range(group_count.bit_length() - 1)
    ]
    team_rows, distances = my_cols[None], [0]
    held, got = [list(remaining)], [swap(picked, "dp", 1)]
    pieces = [
        call(
            block_kernel, "block", shape(1, own_blocks, part_rank, out_width), [VMEM, VMEM, VMEM],
            common_down_factor.T, hidden_input, weighted,
        )
    ]
    orders = [[0]]

    last = []

    def up_step(bit):
        leaving = [k for k in remaining if k & bit]
        value = call(
            functools.partial(pick_kernel, leaving, list(held)), "pick",
            shape(len(leaving), own_blocks, part_rank, out_width), [SMEM, VMEM] + [VMEM] * len(got),
            tenant_of_block, adapter_up_factor, *got,
        )
        last.append(value)
        remaining[:] = [k for k in remaining if not k & bit]
        held.append(list(remaining))
        got.append(swap(value, "dp", bit))

    def block_step(bit):
        value = jnp.concatenate(pieces) if len(pieces) > 1 else pieces[0]
        last.append(value)
        orders.append([k | bit for order in orders for k in order])
        pieces.append(swap(value, "dp", bit))

    up_bits, block_bits = dp_bits[1:], dp_bits[::-1]
    for step, (axis, bit, distance) in enumerate(row_steps):
        new_rows = swap(team_rows, axis, bit)
        if step:
            up_step(up_bits.pop(0))
        block_step(block_bits.pop(0))
        if step == 1:
            to_send, *_ = tie((to_send, team_rows, *last))
        if step == 0:
            team_rows, new_rows, got = tie((team_rows, new_rows, got))
        elif step < len(row_steps) - 1:
            team_rows, new_rows, got, pieces = tie((team_rows, new_rows, got, pieces))
        team_rows = jnp.concatenate([team_rows, new_rows])
        distances = distances + [k | distance for k in distances]
    other_rows = swap(team_rows, "mp", 1)
    weight_slices = lax.all_to_all(
        to_send.reshape(dp_count, features, cols), "dp", split_axis=0, concat_axis=0, tiled=True
    )

    weight_slices, got, pieces = tie((weight_slices, got, pieces))
    if cols % 128:
        slices = weight_slices.transpose(1, 0, 2).reshape(features, 2, part_cols).transpose(1, 0, 2)
    else:
        slices = weight_slices
    frozen = call(
        functools.partial(frozen_kernel, near, distances), "frozen", shape(team, rows, features), [VMEM, VMEM, VMEM],
        team_rows, other_rows, slices, scratch=[pltpu.VMEM((2, features, part_cols), bf16)],
    )
    frozen_mine = lax.all_to_all(
        frozen, ALL, split_axis=0, concat_axis=0, tiled=True, axis_index_groups=teams
    )
    got, pieces, _ = tie((got, pieces, frozen))
    for bit in up_bits:
        up_step(bit)
    for bit in block_bits:
        block_step(bit)
    back_part = call(
        functools.partial(back_kernel, held), "back", shape(part_rank, rows), [SMEM, VMEM, VMEM] + [VMEM] * len(got),
        tenant_of_block, adapter_up_factor, weighted, *got,
    )

    back_rank = lax.all_gather(back_part, "mp", axis=0, tiled=True)

    grad_part = call(
        functools.partial(gradient_kernel, orders, adapter_scale / block_rows), "gradient",
        shape(tenants_here, part_rank, out_width), [SMEM] + [VMEM] * len(pieces), tenant_of_block, *pieces,
    )
    up_factor_gradient = lax.all_gather(grad_part, "mp", axis=1, tiled=True)

    input_gradient = call(
        last_kernel, "last", shape(rows, half_width), [VMEM, VMEM, VMEM],
        frozen_mine, back_rank, common_down_factor.T, out_specs=HBM,
        scratch=[pltpu.VMEM((team, rows, features), bf16), pltpu.SemaphoreType.DMA((team,))],
    )
    return (input_gradient, up_factor_gradient)


def solution(mesh):
    placed = (
        P(("groups", "dp"), None),
        P(("groups", "dp"), None),
        P(("groups", "dp")),
        P("groups"),
        P("mp", "dp"),
        P(),
        P(("groups", "dp"), None, None),
    )
    return jax.shard_map(
        local,
        mesh=mesh,
        in_specs=placed,
        out_specs=(P(("groups", "dp"), "mp"), P(("groups", "dp"), None, None)),
        check_vma=False,
    )
```

```python
import functools
import math

import jax
import jax.numpy as jnp
from jax import lax
from jax.experimental import pallas as pl
from jax.experimental.pallas import tpu as pltpu
from jax.sharding import PartitionSpec as P

adapter_scale = 2.0
ALL = ("groups", "dp", "mp")
f32, bf16 = jnp.float32, jnp.bfloat16
VMEM = pl.BlockSpec(memory_space=pltpu.VMEM)
SMEM = pl.BlockSpec(memory_space=pltpu.SMEM)
HBM = pl.BlockSpec(memory_space=pltpu.HBM)
PARAMS = pltpu.CompilerParams(vmem_limit_bytes=16 * 1024 * 1024)


def place():
    return lax.axis_index("groups"), lax.axis_index("dp"), lax.axis_index("mp")


def piece(index, size):
    return pl.ds(pl.multiple_of(index * size, size), size)


def prepare_kernel(
    leaving, weight, upstream, counts, tenants, up, to_send, weighted, my_cols, picked,
    held_weight, held_upstream, held_counts, held_tenants, held_up, in_sem, out_sem, other_sem,
):
    g, _, m = place()
    copies, depth = to_send.shape[0], to_send.shape[1]
    chunks = in_sem.shape[0]
    size = depth // chunks
    others = [
        pltpu.make_async_copy(source, target, other_sem.at[i])
        for i, (source, target) in enumerate(
            [(counts, held_counts), (upstream, held_upstream), (tenants, held_tenants), (up, held_up)]
        )
    ]
    for load in others:
        load.start()
    loads, stores = [], []
    for c in range(chunks):
        at = pl.ds(pl.multiple_of(g * depth + c * size, size), size)
        loads.append(pltpu.make_async_copy(weight.at[at], held_weight.at[pl.ds(c * size, size)], in_sem.at[c]))
        loads[-1].start()
    rows, part = my_cols.shape
    diagonal = lax.broadcasted_iota(jnp.int32, (rows, rows), 0) == lax.broadcasted_iota(jnp.int32, (rows, rows), 1)
    others[0].wait()
    scale = jnp.where(diagonal, held_counts[...].astype(f32), 0.0).astype(bf16)
    others[1].wait()
    weighted[...] = jnp.dot(scale, held_upstream[...], preferred_element_type=f32).astype(bf16)
    my_cols[...] = weighted[:, piece(m, part)]
    for c in range(chunks):
        loads[c].wait()
        for k in range(copies):
            at = pl.ds(c * size, size)
            stores.append(pltpu.make_async_copy(held_weight.at[at], to_send.at[k, at], out_sem.at[k, c]))
            stores[-1].start()
    others[2].wait()
    others[3].wait()
    for i, k in enumerate(leaving):
        for n in range(picked.shape[1]):
            picked[i, n] = chosen(held_tenants, held_up, k, n, picked.shape[1], picked.shape[2])
    for store in stores:
        store.wait()


def chosen(tenants, up, distance, n, own_blocks, part_rank):
    _, d, m = place()
    wanted = tenants[(d ^ distance) * own_blocks + n] - d * up.shape[0]
    total = jnp.zeros((part_rank, up.shape[2]), bf16)
    for t in range(up.shape[0]):
        total = jnp.where(wanted == t, up[t, piece(m, part_rank)], total)
    return total


def pick_kernel(leaving, held, tenants, up, *refs):
    out = refs[-1]
    for i, k in enumerate(leaving):
        for n in range(out.shape[1]):
            value = chosen(tenants, up, k, n, out.shape[1], out.shape[2])
            for kept, got in zip(held, refs[:-1]):
                value = value + got[kept.index(k), n]
            out[i, n] = value


def both_kernel(leaving, held, tenants, up, *refs):
    out = refs[-1]
    pick_kernel(leaving, held, tenants, up, *refs[: len(held)], out.at[: len(leaving)])
    at = len(leaving)
    for blocks in refs[len(held) : -1]:
        out[at : at + blocks.shape[0]] = blocks[...]
        at += blocks.shape[0]


def back_kernel(held, tenants, up, weighted, *refs):
    out = refs[-1]
    part_rank, rows = out.shape
    own_blocks = refs[0].shape[1]
    size = rows // own_blocks
    for n in range(own_blocks):
        value = chosen(tenants, up, 0, n, own_blocks, part_rank)
        for kept, got in zip(held, refs[:-1]):
            value = value + got[kept.index(0), n]
        at = slice(n * size, (n + 1) * size)
        out[:, at] = lax.dot_general(
            value, weighted[at], (((1,), (1,)), ((), ())), preferred_element_type=f32
        ).astype(bf16)


def block_kernel(down, hidden, weighted, out):
    _, own_blocks, part_rank, _ = out.shape
    size = weighted.shape[0] // own_blocks
    _, _, m = place()
    low = lax.dot_general(
        down[piece(m, part_rank)], hidden[...], (((1,), (1,)), ((), ())), preferred_element_type=f32
    ).astype(bf16)
    for n in range(own_blocks):
        at = slice(n * size, (n + 1) * size)
        out[0, n] = jnp.dot(low[:, at], weighted[at], preferred_element_type=f32).astype(bf16)


def gradient_kernel(orders, scale, tenants, *refs):
    out = refs[-1]
    _, d, _ = place()
    for t in range(out.shape[0]):
        total = jnp.zeros(out.shape[1:], f32)
        for order, got in zip(orders, refs[:-1]):
            own_blocks = got.shape[1]
            for i, k in enumerate(order):
                for n in range(own_blocks if k is not None else 0):
                    wanted = tenants[(d ^ k) * own_blocks + n] - d * out.shape[0]
                    total = total + jnp.where(wanted == t, got[i, n].astype(f32), 0.0)
        out[t] = (total * scale).astype(bf16)


def frozen_kernel(near, distances, mine, other, slices, out, held, ready, sem):
    team, rows, part = mine.shape
    count, features, width = slices.shape
    per_part = count // 2
    g, d, m = place()
    own = g * near + lax.rem(d, near)
    for half in range(2):
        at = lax.rem(m + half, 2) * per_part
        for j in range(per_part):
            held[half, :, j * width : (j + 1) * width] = slices[at + j]
    dims = (((1,), (1,)), ((), ()))
    stores = []
    for c in range(0, team, 2):
        total = lax.dot_general(mine[c : c + 2].reshape(2 * rows, part), held[0], dims, preferred_element_type=f32)
        total += lax.dot_general(other[c : c + 2].reshape(2 * rows, part), held[1], dims, preferred_element_type=f32)
        ready[c : c + 2] = total.astype(bf16).reshape(2, rows, features)
        for k in range(c, c + 2):
            stores.append(pltpu.make_async_copy(ready.at[k], out.at[own ^ distances[k]], sem.at[k]))
            stores[-1].start()
    for store in stores:
        store.wait()


def last_kernel(frozen, back, down, out, held, sem):
    team, rows, features = frozen.shape
    _, _, m = place()
    stores = []
    for k in range(team):
        at = pl.ds(pl.multiple_of(m * (team * features) + k * features, features), features)
        adapter = lax.dot_general(back[...], down[:, at], (((0,), (0,)), ((), ())), preferred_element_type=f32)
        held[k] = (frozen[k].astype(f32) + adapter_scale * adapter).astype(bf16)
        stores.append(pltpu.make_async_copy(held.at[k], out.at[:, pl.ds(k * features, features)], sem.at[k]))
        stores[-1].start()
    for store in stores:
        store.wait()


def local(
    hidden_input,
    upstream,
    rollout_row_counts,
    tenant_of_block,
    frozen_value_weight,
    common_down_factor,
    adapter_up_factor,
):
    group_count = lax.axis_size("groups")
    dp_count = lax.axis_size("dp")
    mp_count = lax.axis_size("mp")
    half_width, cols = frozen_value_weight.shape
    tenants_here, rank, out_width = adapter_up_factor.shape
    part_rank = rank // mp_count
    part_cols = out_width // mp_count
    rows = hidden_input.shape[0]
    own_blocks = tenant_of_block.shape[0] // dp_count
    block_rows = rows // own_blocks

    near = math.gcd(4, dp_count)
    team = group_count * near
    features = half_width // team
    teams = [
        [(gi * dp_count + base + k) * mp_count + mi for gi in range(group_count) for k in range(near)]
        for base in range(0, dp_count, near)
        for mi in range(mp_count)
    ]

    def swap(value, axis, bit):
        size = lax.axis_size(axis)
        return lax.ppermute(value, axis, [(k, k ^ bit) for k in range(size)])

    def shape(*dims):
        return jax.ShapeDtypeStruct(dims, bf16)

    def call(kernel, name, outs, in_specs, *values, scratch=(), out_specs=VMEM, params=PARAMS):
        return pl.pallas_call(
            kernel, in_specs=in_specs, out_specs=out_specs, out_shape=outs, scratch_shapes=list(scratch),
            compiler_params=params, name=name,
        )(*values)

    dp_bits = [1 << k for k in range(dp_count.bit_length() - 1)]
    near_bits = [bit for bit in dp_bits if bit < near]
    tie = lax.optimization_barrier

    repeats = dp_count // near
    leaving = [k for k in range(dp_count) if k & 1]
    remaining = [k for k in range(dp_count) if not k & 1]
    to_send, weighted, my_cols, picked = call(
        functools.partial(prepare_kernel, leaving), "prepare",
        [
            shape(repeats, near * features, cols),
            shape(rows, out_width),
            shape(rows, part_cols),
            shape(len(leaving), own_blocks, part_rank, out_width),
        ],
        [HBM] * 5,
        frozen_value_weight, upstream, rollout_row_counts[None], tenant_of_block, adapter_up_factor,
        out_specs=[HBM, VMEM, VMEM, VMEM],
        params=pltpu.CompilerParams(),
        scratch=[
            pltpu.VMEM((near * features, cols), bf16),
            pltpu.VMEM((rows, out_width), bf16),
            pltpu.VMEM((1, rows), jnp.int32),
            pltpu.SMEM(tenant_of_block.shape, jnp.int32),
            pltpu.VMEM(adapter_up_factor.shape, bf16),
            pltpu.SemaphoreType.DMA((4,)),
            pltpu.SemaphoreType.DMA((repeats, 4)),
            pltpu.SemaphoreType.DMA((4,)),
        ],
    )
    row_steps = [("dp", bit, bit) for bit in near_bits[1:] + near_bits[:1]] + [
        ("groups", 1 << k, near << k) for k in range(group_count.bit_length() - 1)
    ]
    team_rows, distances = my_cols[None], [0]
    held, got = [list(remaining)], [swap(picked, "dp", 1)]
    pieces = [
        call(
            block_kernel, "block", shape(1, own_blocks, part_rank, out_width), [VMEM, VMEM, VMEM],
            common_down_factor.T, hidden_input, weighted,
        )
    ]
    orders = [[0]]

    last = []

    def up_step(bit):
        leaving = [k for k in remaining if k & bit]
        value = call(
            functools.partial(pick_kernel, leaving, list(held)), "pick",
            shape(len(leaving), own_blocks, part_rank, out_width), [SMEM, VMEM] + [VMEM] * len(got),
            tenant_of_block, adapter_up_factor, *got,
        )
        last.append(value)
        remaining[:] = [k for k in remaining if not k & bit]
        held.append(list(remaining))
        got.append(swap(value, "dp", bit))

    def gathered():
        return [k for order in orders for k in order if k is not None]

    def block_step(bit):
        kept = [value[order.count(None) :] for value, order in zip(pieces, orders)]
        value = jnp.concatenate(kept) if len(kept) > 1 else kept[0]
        last.append(value)
        orders.append([k | bit for k in gathered()])
        pieces.append(swap(value, "dp", bit))

    def both_step(bit):
        leaving = [k for k in remaining if k & bit]
        blocks = gathered()
        value = call(
            functools.partial(both_kernel, leaving, list(held)), "both",
            shape(len(leaving) + len(blocks), own_blocks, part_rank, out_width),
            [SMEM, VMEM] + [VMEM] * (len(got) + len(pieces)),
            tenant_of_block, adapter_up_factor, *got, *pieces,
        )
        last.append(value)
        remaining[:] = [k for k in remaining if not k & bit]
        arrived = swap(value, "dp", bit)
        held.append(list(remaining))
        got.append(arrived)
        orders.append([None] * len(leaving) + [k | bit for k in blocks])
        pieces.append(arrived)

    up_bits, block_bits = dp_bits[1:], dp_bits[::-1]
    for step, (axis, bit, distance) in enumerate(row_steps):
        new_rows = swap(team_rows, axis, bit)
        if step == 1 and up_bits[0] == block_bits[0]:
            both_step(up_bits.pop(0))
            block_bits.pop(0)
        else:
            if step:
                up_step(up_bits.pop(0))
            block_step(block_bits.pop(0))
        if step == 1:
            to_send, *_ = tie((to_send, team_rows, *last))
        if step == 0:
            team_rows, new_rows, got = tie((team_rows, new_rows, got))
        elif step < len(row_steps) - 1:
            team_rows, new_rows, got, pieces = tie((team_rows, new_rows, got, pieces))
        team_rows = jnp.concatenate([team_rows, new_rows])
        distances = distances + [k | distance for k in distances]
    other_rows = swap(team_rows, "mp", 1)
    weight_slices = lax.all_to_all(
        to_send.reshape(dp_count, features, cols), "dp", split_axis=0, concat_axis=0, tiled=True
    )

    weight_slices, got, pieces = tie((weight_slices, got, pieces))
    if cols % 128:
        slices = weight_slices.transpose(1, 0, 2).reshape(features, 2, part_cols).transpose(1, 0, 2)
    else:
        slices = weight_slices
    frozen = call(
        functools.partial(frozen_kernel, near, distances), "frozen", shape(team, rows, features), [VMEM, VMEM, VMEM],
        team_rows, other_rows, slices, out_specs=HBM,
        scratch=[
            pltpu.VMEM((2, features, part_cols), bf16),
            pltpu.VMEM((team, rows, features), bf16),
            pltpu.SemaphoreType.DMA((team,)),
        ],
    )
    frozen_mine = lax.all_to_all(
        frozen, ALL, split_axis=0, concat_axis=0, tiled=True, axis_index_groups=teams
    )
    got, pieces, _ = tie((got, pieces, frozen))
    for bit in up_bits:
        up_step(bit)
    for bit in block_bits:
        block_step(bit)
    back_part = call(
        functools.partial(back_kernel, held), "back", shape(part_rank, rows), [SMEM, VMEM, VMEM] + [VMEM] * len(got),
        tenant_of_block, adapter_up_factor, weighted, *got,
    )

    back_rank = lax.all_gather(back_part, "mp", axis=0, tiled=True)

    grad_part = call(
        functools.partial(gradient_kernel, orders, adapter_scale / block_rows), "gradient",
        shape(tenants_here, part_rank, out_width), [SMEM] + [VMEM] * len(pieces), tenant_of_block, *pieces,
    )
    up_factor_gradient = lax.all_gather(grad_part, "mp", axis=1, tiled=True)

    input_gradient = call(
        last_kernel, "last", shape(rows, half_width), [VMEM, VMEM, VMEM],
        frozen_mine, back_rank, common_down_factor.T, out_specs=HBM,
        scratch=[pltpu.VMEM((team, rows, features), bf16), pltpu.SemaphoreType.DMA((team,))],
    )
    return (input_gradient, up_factor_gradient)


def solution(mesh):
    placed = (
        P(("groups", "dp"), None),
        P(("groups", "dp"), None),
        P(("groups", "dp")),
        P("groups"),
        P("mp", "dp"),
        P(),
        P(("groups", "dp"), None, None),
    )
    return jax.shard_map(
        local,
        mesh=mesh,
        in_specs=placed,
        out_specs=(P(("groups", "dp"), "mp"), P(("groups", "dp"), None, None)),
        check_vma=False,
    )
```

```python
import functools
import math

import jax
import jax.numpy as jnp
from jax import lax
from jax.experimental import pallas as pl
from jax.experimental.pallas import tpu as pltpu
from jax.sharding import PartitionSpec as P

adapter_scale = 2.0
ALL = ("groups", "dp", "mp")
f32, bf16 = jnp.float32, jnp.bfloat16
VMEM = pl.BlockSpec(memory_space=pltpu.VMEM)
SMEM = pl.BlockSpec(memory_space=pltpu.SMEM)
HBM = pl.BlockSpec(memory_space=pltpu.HBM)
PARAMS = pltpu.CompilerParams(vmem_limit_bytes=16 * 1024 * 1024)


def place():
    return lax.axis_index("groups"), lax.axis_index("dp"), lax.axis_index("mp")


def piece(index, size):
    return pl.ds(pl.multiple_of(index * size, size), size)


def prepare_kernel(
    leaving, counts, upstream, tenants, up, down, hidden, weighted, my_cols, picked, block,
    held_counts, held_upstream, held_tenants, held_up, held_down, held_hidden, sem,
):
    _, _, m = place()
    _, own_blocks, part_rank, _ = block.shape
    loads = [
        pltpu.make_async_copy(source, target, sem.at[i])
        for i, (source, target) in enumerate(
            [
                (counts, held_counts),
                (upstream, held_upstream),
                (tenants, held_tenants),
                (up, held_up),
                (down.at[piece(m, part_rank)], held_down),
                (hidden, held_hidden),
            ]
        )
    ]
    for load in loads:
        load.start()
    rows, part = my_cols.shape
    diagonal = lax.broadcasted_iota(jnp.int32, (rows, rows), 0) == lax.broadcasted_iota(jnp.int32, (rows, rows), 1)
    loads[0].wait()
    scale = jnp.where(diagonal, held_counts[...].astype(f32), 0.0).astype(bf16)
    loads[1].wait()
    weighted[...] = jnp.dot(scale, held_upstream[...], preferred_element_type=f32).astype(bf16)
    my_cols[...] = weighted[:, piece(m, part)]
    loads[2].wait()
    loads[3].wait()
    for i, k in enumerate(leaving):
        for n in range(own_blocks):
            picked[i, n] = chosen(held_tenants, held_up, k, n, own_blocks, part_rank)
    loads[4].wait()
    loads[5].wait()
    low = lax.dot_general(
        held_down[...], held_hidden[...], (((1,), (1,)), ((), ())), preferred_element_type=f32
    ).astype(bf16)
    size = rows // own_blocks
    for n in range(own_blocks):
        at = slice(n * size, (n + 1) * size)
        block[0, n] = jnp.dot(low[:, at], weighted[at], preferred_element_type=f32).astype(bf16)


def spread_kernel(weight, _, to_send, held, in_sem, out_sem):
    g, _, _ = place()
    copies, depth = to_send.shape[0], to_send.shape[1]
    chunks = in_sem.shape[0]
    size = depth // chunks
    loads, stores = [], []
    for c in range(chunks):
        at = pl.ds(pl.multiple_of(g * depth + c * size, size), size)
        loads.append(pltpu.make_async_copy(weight.at[at], held.at[pl.ds(c * size, size)], in_sem.at[c]))
        loads[-1].start()
    for c in range(chunks):
        loads[c].wait()
        for k in range(copies):
            at = pl.ds(c * size, size)
            stores.append(pltpu.make_async_copy(held.at[at], to_send.at[k, at], out_sem.at[k, c]))
            stores[-1].start()
    for store in stores:
        store.wait()


def chosen(tenants, up, distance, n, own_blocks, part_rank):
    _, d, m = place()
    wanted = tenants[(d ^ distance) * own_blocks + n] - d * up.shape[0]
    total = jnp.zeros((part_rank, up.shape[2]), bf16)
    for t in range(up.shape[0]):
        total = jnp.where(wanted == t, up[t, piece(m, part_rank)], total)
    return total


def pick_kernel(leaving, held, tenants, up, *refs):
    out = refs[-1]
    for i, k in enumerate(leaving):
        for n in range(out.shape[1]):
            value = chosen(tenants, up, k, n, out.shape[1], out.shape[2])
            for kept, got in zip(held, refs[:-1]):
                value = value + got[kept.index(k), n]
            out[i, n] = value


def both_kernel(leaving, held, tenants, up, *refs):
    out = refs[-1]
    pick_kernel(leaving, held, tenants, up, *refs[: len(held)], out.at[: len(leaving)])
    at = len(leaving)
    for blocks in refs[len(held) : -1]:
        out[at : at + blocks.shape[0]] = blocks[...]
        at += blocks.shape[0]


def back_kernel(held, tenants, up, weighted, *refs):
    out = refs[-1]
    part_rank, rows = out.shape
    own_blocks = refs[0].shape[1]
    size = rows // own_blocks
    for n in range(own_blocks):
        value = chosen(tenants, up, 0, n, own_blocks, part_rank)
        for kept, got in zip(held, refs[:-1]):
            value = value + got[kept.index(0), n]
        at = slice(n * size, (n + 1) * size)
        out[:, at] = lax.dot_general(
            value, weighted[at], (((1,), (1,)), ((), ())), preferred_element_type=f32
        ).astype(bf16)


def gradient_kernel(orders, scale, tenants, *refs):
    out = refs[-1]
    _, d, _ = place()
    for t in range(out.shape[0]):
        total = jnp.zeros(out.shape[1:], f32)
        for order, got in zip(orders, refs[:-1]):
            own_blocks = got.shape[1]
            for i, k in enumerate(order):
                for n in range(own_blocks if k is not None else 0):
                    wanted = tenants[(d ^ k) * own_blocks + n] - d * out.shape[0]
                    total = total + jnp.where(wanted == t, got[i, n].astype(f32), 0.0)
        out[t] = (total * scale).astype(bf16)


def frozen_kernel(near, distances, mine, other, slices, out, held, ready, sem):
    team, rows, part = mine.shape
    count, features, width = slices.shape
    per_part = count // 2
    g, d, m = place()
    own = g * near + lax.rem(d, near)
    for half in range(2):
        at = lax.rem(m + half, 2) * per_part
        for j in range(per_part):
            held[half, :, j * width : (j + 1) * width] = slices[at + j]
    dims = (((1,), (1,)), ((), ()))
    stores = []
    for c in range(0, team, 2):
        total = lax.dot_general(mine[c : c + 2].reshape(2 * rows, part), held[0], dims, preferred_element_type=f32)
        total += lax.dot_general(other[c : c + 2].reshape(2 * rows, part), held[1], dims, preferred_element_type=f32)
        ready[c : c + 2] = total.astype(bf16).reshape(2, rows, features)
        for k in range(c, c + 2):
            stores.append(pltpu.make_async_copy(ready.at[k], out.at[own ^ distances[k]], sem.at[k]))
            stores[-1].start()
    for store in stores:
        store.wait()


def last_kernel(frozen, back, down, out, held, sem):
    team, rows, features = frozen.shape
    _, _, m = place()
    stores = []
    for k in range(team):
        at = pl.ds(pl.multiple_of(m * (team * features) + k * features, features), features)
        adapter = lax.dot_general(back[...], down[:, at], (((0,), (0,)), ((), ())), preferred_element_type=f32)
        held[k] = (frozen[k].astype(f32) + adapter_scale * adapter).astype(bf16)
        stores.append(pltpu.make_async_copy(held.at[k], out.at[:, pl.ds(k * features, features)], sem.at[k]))
        stores[-1].start()
    for store in stores:
        store.wait()


def local(
    hidden_input,
    upstream,
    rollout_row_counts,
    tenant_of_block,
    frozen_value_weight,
    common_down_factor,
    adapter_up_factor,
):
    group_count = lax.axis_size("groups")
    dp_count = lax.axis_size("dp")
    mp_count = lax.axis_size("mp")
    half_width, cols = frozen_value_weight.shape
    tenants_here, rank, out_width = adapter_up_factor.shape
    part_rank = rank // mp_count
    part_cols = out_width // mp_count
    rows = hidden_input.shape[0]
    own_blocks = tenant_of_block.shape[0] // dp_count
    block_rows = rows // own_blocks

    near = math.gcd(4, dp_count)
    team = group_count * near
    features = half_width // team
    teams = [
        [(gi * dp_count + base + k) * mp_count + mi for gi in range(group_count) for k in range(near)]
        for base in range(0, dp_count, near)
        for mi in range(mp_count)
    ]

    def swap(value, axis, bit):
        size = lax.axis_size(axis)
        return lax.ppermute(value, axis, [(k, k ^ bit) for k in range(size)])

    def shape(*dims):
        return jax.ShapeDtypeStruct(dims, bf16)

    def call(kernel, name, outs, in_specs, *values, scratch=(), out_specs=VMEM, params=PARAMS):
        return pl.pallas_call(
            kernel, in_specs=in_specs, out_specs=out_specs, out_shape=outs, scratch_shapes=list(scratch),
            compiler_params=params, name=name,
        )(*values)

    dp_bits = [1 << k for k in range(dp_count.bit_length() - 1)]
    near_bits = [bit for bit in dp_bits if bit < near]
    tie = lax.optimization_barrier

    repeats = dp_count // near
    leaving = [k for k in range(dp_count) if k & 1]
    remaining = [k for k in range(dp_count) if not k & 1]
    weighted, my_cols, picked, block = call(
        functools.partial(prepare_kernel, leaving), "prepare",
        [
            shape(rows, out_width),
            shape(rows, part_cols),
            shape(len(leaving), own_blocks, part_rank, out_width),
            shape(1, own_blocks, part_rank, out_width),
        ],
        [HBM] * 6, rollout_row_counts[None], upstream, tenant_of_block, adapter_up_factor, common_down_factor.T,
        hidden_input, out_specs=[VMEM] * 4, params=pltpu.CompilerParams(),
        scratch=[
            pltpu.VMEM((1, rows), jnp.int32),
            pltpu.VMEM((rows, out_width), bf16),
            pltpu.SMEM(tenant_of_block.shape, jnp.int32),
            pltpu.VMEM(adapter_up_factor.shape, bf16),
            pltpu.VMEM((part_rank, common_down_factor.shape[0]), bf16),
            pltpu.VMEM(hidden_input.shape, bf16),
            pltpu.SemaphoreType.DMA((6,)),
        ],
    )
    to_send = call(
        spread_kernel, "spread", shape(repeats, near * features, cols), [HBM] * 2, frozen_value_weight, block,
        out_specs=HBM, params=pltpu.CompilerParams(),
        scratch=[
            pltpu.VMEM((near * features, cols), bf16),
            pltpu.SemaphoreType.DMA((4,)),
            pltpu.SemaphoreType.DMA((repeats, 4)),
        ],
    )
    row_steps = [("dp", bit, bit) for bit in near_bits[1:] + near_bits[:1]] + [
        ("groups", 1 << k, near << k) for k in range(group_count.bit_length() - 1)
    ]
    team_rows, distances = my_cols[None], [0]
    held, got = [list(remaining)], [swap(picked, "dp", 1)]
    pieces, orders = [block], [[0]]
    last = []

    def up_step(bit):
        leaving = [k for k in remaining if k & bit]
        value = call(
            functools.partial(pick_kernel, leaving, list(held)), "pick",
            shape(len(leaving), own_blocks, part_rank, out_width), [SMEM, VMEM] + [VMEM] * len(got),
            tenant_of_block, adapter_up_factor, *got,
        )
        last.append(value)
        remaining[:] = [k for k in remaining if not k & bit]
        held.append(list(remaining))
        got.append(swap(value, "dp", bit))

    def gathered():
        return [k for order in orders for k in order if k is not None]

    def block_step(bit):
        kept = [value[order.count(None) :] for value, order in zip(pieces, orders)]
        value = jnp.concatenate(kept) if len(kept) > 1 else kept[0]
        last.append(value)
        orders.append([k | bit for k in gathered()])
        pieces.append(swap(value, "dp", bit))

    def both_step(bit):
        leaving = [k for k in remaining if k & bit]
        blocks = gathered()
        value = call(
            functools.partial(both_kernel, leaving, list(held)), "both",
            shape(len(leaving) + len(blocks), own_blocks, part_rank, out_width),
            [SMEM, VMEM] + [VMEM] * (len(got) + len(pieces)),
            tenant_of_block, adapter_up_factor, *got, *pieces,
        )
        last.append(value)
        remaining[:] = [k for k in remaining if not k & bit]
        arrived = swap(value, "dp", bit)
        held.append(list(remaining))
        got.append(arrived)
        orders.append([None] * len(leaving) + [k | bit for k in blocks])
        pieces.append(arrived)

    up_bits, block_bits = dp_bits[1:], dp_bits[::-1]
    for step, (axis, bit, distance) in enumerate(row_steps):
        new_rows = swap(team_rows, axis, bit)
        if step == 1 and up_bits[0] == block_bits[0]:
            both_step(up_bits.pop(0))
            block_bits.pop(0)
        else:
            if step:
                up_step(up_bits.pop(0))
            block_step(block_bits.pop(0))
        if step == 1:
            to_send, *_ = tie((to_send, team_rows, *last))
        if step == 0:
            team_rows, new_rows, got, to_send = tie((team_rows, new_rows, got, to_send))
        elif step < len(row_steps) - 1:
            team_rows, new_rows, got, pieces = tie((team_rows, new_rows, got, pieces))
        team_rows = jnp.concatenate([team_rows, new_rows])
        distances = distances + [k | distance for k in distances]
    other_rows = swap(team_rows, "mp", 1)
    weight_slices = lax.all_to_all(
        to_send.reshape(dp_count, features, cols), "dp", split_axis=0, concat_axis=0, tiled=True
    )

    weight_slices, _ = tie((weight_slices, last))
    if cols % 128:
        slices = weight_slices.transpose(1, 0, 2).reshape(features, 2, part_cols).transpose(1, 0, 2)
    else:
        slices = weight_slices
    frozen = call(
        functools.partial(frozen_kernel, near, distances), "frozen", shape(team, rows, features), [VMEM, VMEM, VMEM],
        team_rows, other_rows, slices, out_specs=HBM,
        scratch=[
            pltpu.VMEM((2, features, part_cols), bf16),
            pltpu.VMEM((team, rows, features), bf16),
            pltpu.SemaphoreType.DMA((team,)),
        ],
    )
    frozen, got, pieces = tie((frozen, got, pieces))
    frozen_mine = lax.all_to_all(
        frozen, ALL, split_axis=0, concat_axis=0, tiled=True, axis_index_groups=teams
    )
    for bit in up_bits:
        up_step(bit)
    for bit in block_bits:
        block_step(bit)
    back_part = call(
        functools.partial(back_kernel, held), "back", shape(part_rank, rows), [SMEM, VMEM, VMEM] + [VMEM] * len(got),
        tenant_of_block, adapter_up_factor, weighted, *got,
    )

    back_rank = lax.all_gather(back_part, "mp", axis=0, tiled=True)

    grad_part = call(
        functools.partial(gradient_kernel, orders, adapter_scale / block_rows), "gradient",
        shape(tenants_here, part_rank, out_width), [SMEM] + [VMEM] * len(pieces), tenant_of_block, *pieces,
    )
    up_factor_gradient = lax.all_gather(grad_part, "mp", axis=1, tiled=True)

    input_gradient = call(
        last_kernel, "last", shape(rows, half_width), [VMEM, VMEM, VMEM],
        frozen_mine, back_rank, common_down_factor.T, out_specs=HBM,
        scratch=[pltpu.VMEM((team, rows, features), bf16), pltpu.SemaphoreType.DMA((team,))],
    )
    return (input_gradient, up_factor_gradient)


def solution(mesh):
    placed = (
        P(("groups", "dp"), None),
        P(("groups", "dp"), None),
        P(("groups", "dp")),
        P("groups"),
        P("mp", "dp"),
        P(),
        P(("groups", "dp"), None, None),
    )
    return jax.shard_map(
        local,
        mesh=mesh,
        in_specs=placed,
        out_specs=(P(("groups", "dp"), "mp"), P(("groups", "dp"), None, None)),
        check_vma=False,
    )
```

```python
import functools
import math

import jax
import jax.numpy as jnp
from jax import lax
from jax.experimental import pallas as pl
from jax.experimental.pallas import tpu as pltpu
from jax.sharding import PartitionSpec as P

adapter_scale = 2.0
ALL = ("groups", "dp", "mp")
f32, bf16 = jnp.float32, jnp.bfloat16
VMEM = pl.BlockSpec(memory_space=pltpu.VMEM)
SMEM = pl.BlockSpec(memory_space=pltpu.SMEM)
HBM = pl.BlockSpec(memory_space=pltpu.HBM)
PARAMS = pltpu.CompilerParams(vmem_limit_bytes=16 * 1024 * 1024)


def place():
    return lax.axis_index("groups"), lax.axis_index("dp"), lax.axis_index("mp")


def piece(index, size):
    return pl.ds(pl.multiple_of(index * size, size), size)


def prepare_kernel(
    leaving, counts, upstream, tenants, up, down, hidden, weighted, my_cols, picked, block,
    held_counts, held_upstream, held_tenants, held_up, held_down, held_hidden, sem,
):
    _, _, m = place()
    _, own_blocks, part_rank, _ = block.shape
    loads = [
        pltpu.make_async_copy(source, target, sem.at[i])
        for i, (source, target) in enumerate(
            [
                (counts, held_counts),
                (upstream, held_upstream),
                (tenants, held_tenants),
                (up, held_up),
                (down.at[piece(m, part_rank)], held_down),
                (hidden, held_hidden),
            ]
        )
    ]
    for load in loads:
        load.start()
    rows, part = my_cols.shape
    diagonal = lax.broadcasted_iota(jnp.int32, (rows, rows), 0) == lax.broadcasted_iota(jnp.int32, (rows, rows), 1)
    loads[0].wait()
    scale = jnp.where(diagonal, held_counts[...].astype(f32), 0.0).astype(bf16)
    loads[1].wait()
    weighted[...] = jnp.dot(scale, held_upstream[...], preferred_element_type=f32).astype(bf16)
    my_cols[...] = weighted[:, piece(m, part)]
    loads[2].wait()
    loads[3].wait()
    for i, k in enumerate(leaving):
        for n in range(own_blocks):
            picked[i, n] = chosen(held_tenants, held_up, k, n, own_blocks, part_rank)
    loads[4].wait()
    loads[5].wait()
    low = lax.dot_general(
        held_down[...], held_hidden[...], (((1,), (1,)), ((), ())), preferred_element_type=f32
    ).astype(bf16)
    size = rows // own_blocks
    for n in range(own_blocks):
        at = slice(n * size, (n + 1) * size)
        block[0, n] = jnp.dot(low[:, at], weighted[at], preferred_element_type=f32).astype(bf16)


def spread_kernel(weight, _, to_send, held, in_sem, out_sem):
    g, _, _ = place()
    copies, depth = to_send.shape[0], to_send.shape[1]
    chunks = in_sem.shape[0]
    size = depth // chunks
    loads, stores = [], []
    for c in range(chunks):
        at = pl.ds(pl.multiple_of(g * depth + c * size, size), size)
        loads.append(pltpu.make_async_copy(weight.at[at], held.at[pl.ds(c * size, size)], in_sem.at[c]))
        loads[-1].start()
    for c in range(chunks):
        loads[c].wait()
        for k in range(copies):
            at = pl.ds(c * size, size)
            stores.append(pltpu.make_async_copy(held.at[at], to_send.at[k, at], out_sem.at[k, c]))
            stores[-1].start()
    for store in stores:
        store.wait()


def chosen(tenants, up, distance, n, own_blocks, part_rank):
    _, d, m = place()
    wanted = tenants[(d ^ distance) * own_blocks + n] - d * up.shape[0]
    total = jnp.zeros((part_rank, up.shape[2]), bf16)
    for t in range(up.shape[0]):
        total = jnp.where(wanted == t, up[t, piece(m, part_rank)], total)
    return total


def pick_kernel(leaving, held, tenants, up, *refs):
    out = refs[-1]
    for i, k in enumerate(leaving):
        for n in range(out.shape[1]):
            value = chosen(tenants, up, k, n, out.shape[1], out.shape[2])
            for kept, got in zip(held, refs[:-1]):
                value = value + got[kept.index(k), n]
            out[i, n] = value


def both_kernel(leaving, held, tenants, up, *refs):
    out = refs[-1]
    pick_kernel(leaving, held, tenants, up, *refs[: len(held)], out.at[: len(leaving)])
    at = len(leaving)
    for blocks in refs[len(held) : -1]:
        out[at : at + blocks.shape[0]] = blocks[...]
        at += blocks.shape[0]


def back_kernel(held, tenants, up, weighted, *refs):
    out = refs[-1]
    part_rank, rows = out.shape
    own_blocks = refs[0].shape[1]
    size = rows // own_blocks
    for n in range(own_blocks):
        value = chosen(tenants, up, 0, n, own_blocks, part_rank)
        for kept, got in zip(held, refs[:-1]):
            value = value + got[kept.index(0), n]
        at = slice(n * size, (n + 1) * size)
        out[:, at] = lax.dot_general(
            value, weighted[at], (((1,), (1,)), ((), ())), preferred_element_type=f32
        ).astype(bf16)


def gradient_kernel(orders, scale, tenants, *refs):
    out = refs[-1]
    _, d, _ = place()
    for t in range(out.shape[0]):
        total = jnp.zeros(out.shape[1:], f32)
        for order, got in zip(orders, refs[:-1]):
            own_blocks = got.shape[1]
            for i, k in enumerate(order):
                for n in range(own_blocks if k is not None else 0):
                    wanted = tenants[(d ^ k) * own_blocks + n] - d * out.shape[0]
                    total = total + jnp.where(wanted == t, got[i, n].astype(f32), 0.0)
        out[t] = (total * scale).astype(bf16)


def frozen_kernel(near, distances, mine, other, slices, out, held, ready, sem):
    team, rows, part = mine.shape
    count, features, width = slices.shape
    per_part = count // 2
    g, d, m = place()
    own = g * near + lax.rem(d, near)
    for half in range(2):
        at = lax.rem(m + half, 2) * per_part
        for j in range(per_part):
            held[half, :, j * width : (j + 1) * width] = slices[at + j]
    dims = (((1,), (1,)), ((), ()))
    stores = []
    for c in range(0, team, 2):
        total = lax.dot_general(mine[c : c + 2].reshape(2 * rows, part), held[0], dims, preferred_element_type=f32)
        total += lax.dot_general(other[c : c + 2].reshape(2 * rows, part), held[1], dims, preferred_element_type=f32)
        ready[c : c + 2] = total.astype(bf16).reshape(2, rows, features)
        for k in range(c, c + 2):
            stores.append(pltpu.make_async_copy(ready.at[k], out.at[own ^ distances[k]], sem.at[k]))
            stores[-1].start()
    for store in stores:
        store.wait()


def last_kernel(frozen, mine, other, down, gradient, other_gradient, out, whole, back, held, sem, gradient_sem):
    team, rows, features = frozen.shape
    part_rank, _ = mine.shape
    _, _, m = place()
    stores = [
        pltpu.make_async_copy(gradient, whole.at[:, piece(m, part_rank)], gradient_sem.at[0]),
        pltpu.make_async_copy(other_gradient, whole.at[:, piece(1 - m, part_rank)], gradient_sem.at[1]),
    ]
    for store in stores:
        store.start()
    back[piece(m, part_rank)] = mine[...]
    back[piece(1 - m, part_rank)] = other[...]
    for k in range(team):
        at = pl.ds(pl.multiple_of(m * (team * features) + k * features, features), features)
        adapter = lax.dot_general(back[...], down[:, at], (((0,), (0,)), ((), ())), preferred_element_type=f32)
        held[k] = (frozen[k].astype(f32) + adapter_scale * adapter).astype(bf16)
        stores.append(pltpu.make_async_copy(held.at[k], out.at[:, pl.ds(k * features, features)], sem.at[k]))
        stores[-1].start()
    for store in stores:
        store.wait()


def local(
    hidden_input,
    upstream,
    rollout_row_counts,
    tenant_of_block,
    frozen_value_weight,
    common_down_factor,
    adapter_up_factor,
):
    group_count = lax.axis_size("groups")
    dp_count = lax.axis_size("dp")
    mp_count = lax.axis_size("mp")
    half_width, cols = frozen_value_weight.shape
    tenants_here, rank, out_width = adapter_up_factor.shape
    part_rank = rank // mp_count
    part_cols = out_width // mp_count
    rows = hidden_input.shape[0]
    own_blocks = tenant_of_block.shape[0] // dp_count
    block_rows = rows // own_blocks

    near = math.gcd(4, dp_count)
    team = group_count * near
    features = half_width // team
    teams = [
        [(gi * dp_count + base + k) * mp_count + mi for gi in range(group_count) for k in range(near)]
        for base in range(0, dp_count, near)
        for mi in range(mp_count)
    ]

    def swap(value, axis, bit):
        size = lax.axis_size(axis)
        return lax.ppermute(value, axis, [(k, k ^ bit) for k in range(size)])

    def shape(*dims):
        return jax.ShapeDtypeStruct(dims, bf16)

    def call(kernel, name, outs, in_specs, *values, scratch=(), out_specs=VMEM, params=PARAMS):
        return pl.pallas_call(
            kernel, in_specs=in_specs, out_specs=out_specs, out_shape=outs, scratch_shapes=list(scratch),
            compiler_params=params, name=name,
        )(*values)

    dp_bits = [1 << k for k in range(dp_count.bit_length() - 1)]
    near_bits = [bit for bit in dp_bits if bit < near]
    tie = lax.optimization_barrier

    repeats = dp_count // near
    leaving = [k for k in range(dp_count) if k & 1]
    remaining = [k for k in range(dp_count) if not k & 1]
    weighted, my_cols, picked, block = call(
        functools.partial(prepare_kernel, leaving), "prepare",
        [
            shape(rows, out_width),
            shape(rows, part_cols),
            shape(len(leaving), own_blocks, part_rank, out_width),
            shape(1, own_blocks, part_rank, out_width),
        ],
        [HBM] * 6, rollout_row_counts[None], upstream, tenant_of_block, adapter_up_factor, common_down_factor.T,
        hidden_input, out_specs=[VMEM] * 4, params=pltpu.CompilerParams(),
        scratch=[
            pltpu.VMEM((1, rows), jnp.int32),
            pltpu.VMEM((rows, out_width), bf16),
            pltpu.SMEM(tenant_of_block.shape, jnp.int32),
            pltpu.VMEM(adapter_up_factor.shape, bf16),
            pltpu.VMEM((part_rank, common_down_factor.shape[0]), bf16),
            pltpu.VMEM(hidden_input.shape, bf16),
            pltpu.SemaphoreType.DMA((6,)),
        ],
    )
    to_send = call(
        spread_kernel, "spread", shape(repeats, near * features, cols), [HBM] * 2, frozen_value_weight, block,
        out_specs=HBM, params=pltpu.CompilerParams(),
        scratch=[
            pltpu.VMEM((near * features, cols), bf16),
            pltpu.SemaphoreType.DMA((4,)),
            pltpu.SemaphoreType.DMA((repeats, 4)),
        ],
    )
    row_steps = [("dp", bit, bit) for bit in near_bits[1:] + near_bits[:1]] + [
        ("groups", 1 << k, near << k) for k in range(group_count.bit_length() - 1)
    ]
    team_rows, distances = my_cols[None], [0]
    held, got = [list(remaining)], [swap(picked, "dp", 1)]
    pieces, orders = [block], [[0]]
    last = []

    def up_step(bit):
        leaving = [k for k in remaining if k & bit]
        value = call(
            functools.partial(pick_kernel, leaving, list(held)), "pick",
            shape(len(leaving), own_blocks, part_rank, out_width), [SMEM, VMEM] + [VMEM] * len(got),
            tenant_of_block, adapter_up_factor, *got,
        )
        last.append(value)
        remaining[:] = [k for k in remaining if not k & bit]
        held.append(list(remaining))
        got.append(swap(value, "dp", bit))

    def gathered():
        return [k for order in orders for k in order if k is not None]

    def block_step(bit):
        kept = [value[order.count(None) :] for value, order in zip(pieces, orders)]
        value = jnp.concatenate(kept) if len(kept) > 1 else kept[0]
        last.append(value)
        orders.append([k | bit for k in gathered()])
        pieces.append(swap(value, "dp", bit))

    def both_step(bit):
        leaving = [k for k in remaining if k & bit]
        blocks = gathered()
        value = call(
            functools.partial(both_kernel, leaving, list(held)), "both",
            shape(len(leaving) + len(blocks), own_blocks, part_rank, out_width),
            [SMEM, VMEM] + [VMEM] * (len(got) + len(pieces)),
            tenant_of_block, adapter_up_factor, *got, *pieces,
        )
        last.append(value)
        remaining[:] = [k for k in remaining if not k & bit]
        arrived = swap(value, "dp", bit)
        held.append(list(remaining))
        got.append(arrived)
        orders.append([None] * len(leaving) + [k | bit for k in blocks])
        pieces.append(arrived)

    up_bits, block_bits = dp_bits[1:], dp_bits[::-1]
    for step, (axis, bit, distance) in enumerate(row_steps):
        new_rows = swap(team_rows, axis, bit)
        if step == 1 and up_bits[0] == block_bits[0]:
            both_step(up_bits.pop(0))
            block_bits.pop(0)
        else:
            if step:
                up_step(up_bits.pop(0))
            block_step(block_bits.pop(0))
        if step == 1:
            to_send, *_ = tie((to_send, team_rows, *last))
        if step == 0:
            team_rows, new_rows, got, to_send = tie((team_rows, new_rows, got, to_send))
        elif step < len(row_steps) - 1:
            team_rows, new_rows, got, pieces = tie((team_rows, new_rows, got, pieces))
        team_rows = jnp.concatenate([team_rows, new_rows])
        distances = distances + [k | distance for k in distances]
    other_rows = swap(team_rows, "mp", 1)
    weight_slices = lax.all_to_all(
        to_send.reshape(dp_count, features, cols), "dp", split_axis=0, concat_axis=0, tiled=True
    )

    weight_slices, _ = tie((weight_slices, last))
    if cols % 128:
        slices = weight_slices.transpose(1, 0, 2).reshape(features, 2, part_cols).transpose(1, 0, 2)
    else:
        slices = weight_slices
    frozen = call(
        functools.partial(frozen_kernel, near, distances), "frozen", shape(team, rows, features), [VMEM, VMEM, VMEM],
        team_rows, other_rows, slices, out_specs=HBM,
        scratch=[
            pltpu.VMEM((2, features, part_cols), bf16),
            pltpu.VMEM((team, rows, features), bf16),
            pltpu.SemaphoreType.DMA((team,)),
        ],
    )
    frozen, got, pieces = tie((frozen, got, pieces))
    frozen_mine = lax.all_to_all(
        frozen, ALL, split_axis=0, concat_axis=0, tiled=True, axis_index_groups=teams
    )
    for bit in up_bits:
        up_step(bit)
    for bit in block_bits:
        block_step(bit)
    back_part = call(
        functools.partial(back_kernel, held), "back", shape(part_rank, rows), [SMEM, VMEM, VMEM] + [VMEM] * len(got),
        tenant_of_block, adapter_up_factor, weighted, *got,
    )

    grad_part = call(
        functools.partial(gradient_kernel, orders, adapter_scale / block_rows), "gradient",
        shape(tenants_here, part_rank, out_width), [SMEM] + [VMEM] * len(pieces), tenant_of_block, *pieces,
    )
    input_gradient, up_factor_gradient = call(
        last_kernel, "last", [shape(rows, half_width), shape(*adapter_up_factor.shape)], [VMEM] * 6,
        frozen_mine, back_part, swap(back_part, "mp", 1), common_down_factor.T, grad_part, swap(grad_part, "mp", 1),
        out_specs=[HBM, HBM],
        scratch=[
            pltpu.VMEM((rank, rows), bf16),
            pltpu.VMEM((team, rows, features), bf16),
            pltpu.SemaphoreType.DMA((team,)),
            pltpu.SemaphoreType.DMA((2,)),
        ],
    )
    return (input_gradient, up_factor_gradient)


def solution(mesh):
    placed = (
        P(("groups", "dp"), None),
        P(("groups", "dp"), None),
        P(("groups", "dp")),
        P("groups"),
        P("mp", "dp"),
        P(),
        P(("groups", "dp"), None, None),
    )
    return jax.shard_map(
        local,
        mesh=mesh,
        in_specs=placed,
        out_specs=(P(("groups", "dp"), "mp"), P(("groups", "dp"), None, None)),
        check_vma=False,
    )
```

```python
import functools
import math

import jax
import jax.numpy as jnp
from jax import lax
from jax.experimental import pallas as pl
from jax.experimental.pallas import tpu as pltpu
from jax.sharding import PartitionSpec as P

adapter_scale = 2.0
ALL = ("groups", "dp", "mp")
f32, bf16 = jnp.float32, jnp.bfloat16
VMEM = pl.BlockSpec(memory_space=pltpu.VMEM)
SMEM = pl.BlockSpec(memory_space=pltpu.SMEM)
HBM = pl.BlockSpec(memory_space=pltpu.HBM)
PARAMS = pltpu.CompilerParams(vmem_limit_bytes=16 * 1024 * 1024)


def place():
    return lax.axis_index("groups"), lax.axis_index("dp"), lax.axis_index("mp")


def piece(index, size):
    return pl.ds(pl.multiple_of(index * size, size), size)


def prepare_kernel(
    leaving, counts, upstream, tenants, up, down, hidden, weighted, my_cols, sooner, later, block,
    held_counts, held_upstream, held_tenants, held_up, held_down, held_hidden, sem,
):
    _, _, m = place()
    _, own_blocks, part_rank, _ = block.shape
    loads = [
        pltpu.make_async_copy(source, target, sem.at[i])
        for i, (source, target) in enumerate(
            [
                (counts, held_counts),
                (upstream, held_upstream),
                (tenants, held_tenants),
                (up, held_up),
                (down.at[piece(m, part_rank)], held_down),
                (hidden, held_hidden),
            ]
        )
    ]
    for load in loads:
        load.start()
    rows, part = my_cols.shape
    diagonal = lax.broadcasted_iota(jnp.int32, (rows, rows), 0) == lax.broadcasted_iota(jnp.int32, (rows, rows), 1)
    loads[0].wait()
    scale = jnp.where(diagonal, held_counts[...].astype(f32), 0.0).astype(bf16)
    loads[1].wait()
    weighted[...] = jnp.dot(scale, held_upstream[...], preferred_element_type=f32).astype(bf16)
    my_cols[...] = weighted[:, piece(m, part)]
    loads[2].wait()
    loads[3].wait()
    for ks, picked in zip(leaving, (sooner, later)):
        for i, k in enumerate(ks):
            for n in range(own_blocks):
                picked[i, n] = chosen(held_tenants, held_up, k, n, own_blocks, part_rank)
    loads[4].wait()
    loads[5].wait()
    low = lax.dot_general(
        held_down[...], held_hidden[...], (((1,), (1,)), ((), ())), preferred_element_type=f32
    ).astype(bf16)
    size = rows // own_blocks
    for n in range(own_blocks):
        at = slice(n * size, (n + 1) * size)
        block[0, n] = jnp.dot(low[:, at], weighted[at], preferred_element_type=f32).astype(bf16)


def spread_kernel(weight, _, to_send, held, in_sem, out_sem):
    g, _, _ = place()
    copies, depth = to_send.shape[0], to_send.shape[1]
    chunks = in_sem.shape[0]
    size = depth // chunks
    loads, stores = [], []
    for c in range(chunks):
        at = pl.ds(pl.multiple_of(g * depth + c * size, size), size)
        loads.append(pltpu.make_async_copy(weight.at[at], held.at[pl.ds(c * size, size)], in_sem.at[c]))
        loads[-1].start()
    for c in range(chunks):
        loads[c].wait()
        for k in range(copies):
            at = pl.ds(c * size, size)
            stores.append(pltpu.make_async_copy(held.at[at], to_send.at[k, at], out_sem.at[k, c]))
            stores[-1].start()
    for store in stores:
        store.wait()


def chosen(tenants, up, distance, n, own_blocks, part_rank):
    _, d, m = place()
    wanted = tenants[(d ^ distance) * own_blocks + n] - d * up.shape[0]
    total = jnp.zeros((part_rank, up.shape[2]), bf16)
    for t in range(up.shape[0]):
        total = jnp.where(wanted == t, up[t, piece(m, part_rank)], total)
    return total


def pick_kernel(leaving, held, tenants, up, *refs):
    out = refs[-1]
    for i, k in enumerate(leaving):
        for n in range(out.shape[1]):
            value = chosen(tenants, up, k, n, out.shape[1], out.shape[2])
            for kept, got in zip(held, refs[:-1]):
                if k in kept:
                    value = value + got[kept.index(k), n]
            out[i, n] = value


def both_kernel(leaving, held, tenants, up, *refs):
    out = refs[-1]
    pick_kernel(leaving, held, tenants, up, *refs[: len(held)], out.at[: len(leaving)])
    at = len(leaving)
    for blocks in refs[len(held) : -1]:
        out[at : at + blocks.shape[0]] = blocks[...]
        at += blocks.shape[0]


def back_kernel(held, tenants, up, weighted, *refs):
    out = refs[-1]
    part_rank, rows = out.shape
    own_blocks = refs[0].shape[1]
    size = rows // own_blocks
    for n in range(own_blocks):
        value = chosen(tenants, up, 0, n, own_blocks, part_rank)
        for kept, got in zip(held, refs[:-1]):
            if 0 in kept:
                value = value + got[kept.index(0), n]
        at = slice(n * size, (n + 1) * size)
        out[:, at] = lax.dot_general(
            value, weighted[at], (((1,), (1,)), ((), ())), preferred_element_type=f32
        ).astype(bf16)


def gradient_kernel(orders, scale, tenants, *refs):
    out = refs[-1]
    _, d, _ = place()
    for t in range(out.shape[0]):
        total = jnp.zeros(out.shape[1:], f32)
        for order, got in zip(orders, refs[:-1]):
            own_blocks = got.shape[1]
            for i, k in enumerate(order):
                for n in range(own_blocks if k is not None else 0):
                    wanted = tenants[(d ^ k) * own_blocks + n] - d * out.shape[0]
                    total = total + jnp.where(wanted == t, got[i, n].astype(f32), 0.0)
        out[t] = (total * scale).astype(bf16)


def frozen_kernel(near, distances, mine, other, slices, out, held, ready, sem):
    team, rows, part = mine.shape
    count, features, width = slices.shape
    per_part = count // 2
    g, d, m = place()
    own = g * near + lax.rem(d, near)
    for half in range(2):
        at = lax.rem(m + half, 2) * per_part
        for j in range(per_part):
            held[half, :, j * width : (j + 1) * width] = slices[at + j]
    dims = (((1,), (1,)), ((), ()))
    stores = []
    for c in range(0, team, 2):
        total = lax.dot_general(mine[c : c + 2].reshape(2 * rows, part), held[0], dims, preferred_element_type=f32)
        total += lax.dot_general(other[c : c + 2].reshape(2 * rows, part), held[1], dims, preferred_element_type=f32)
        ready[c : c + 2] = total.astype(bf16).reshape(2, rows, features)
        for k in range(c, c + 2):
            stores.append(pltpu.make_async_copy(ready.at[k], out.at[own ^ distances[k]], sem.at[k]))
            stores[-1].start()
    for store in stores:
        store.wait()


def last_kernel(frozen, mine, other, down, gradient, other_gradient, out, whole, back, held, sem, gradient_sem):
    team, rows, features = frozen.shape
    part_rank, _ = mine.shape
    _, _, m = place()
    stores = [
        pltpu.make_async_copy(gradient, whole.at[:, piece(m, part_rank)], gradient_sem.at[0]),
        pltpu.make_async_copy(other_gradient, whole.at[:, piece(1 - m, part_rank)], gradient_sem.at[1]),
    ]
    for store in stores:
        store.start()
    back[piece(m, part_rank)] = mine[...]
    back[piece(1 - m, part_rank)] = other[...]
    for k in range(team):
        at = pl.ds(pl.multiple_of(m * (team * features) + k * features, features), features)
        adapter = lax.dot_general(back[...], down[:, at], (((0,), (0,)), ((), ())), preferred_element_type=f32)
        held[k] = (frozen[k].astype(f32) + adapter_scale * adapter).astype(bf16)
        stores.append(pltpu.make_async_copy(held.at[k], out.at[:, pl.ds(k * features, features)], sem.at[k]))
        stores[-1].start()
    for store in stores:
        store.wait()


def local(
    hidden_input,
    upstream,
    rollout_row_counts,
    tenant_of_block,
    frozen_value_weight,
    common_down_factor,
    adapter_up_factor,
):
    group_count = lax.axis_size("groups")
    dp_count = lax.axis_size("dp")
    mp_count = lax.axis_size("mp")
    half_width, cols = frozen_value_weight.shape
    tenants_here, rank, out_width = adapter_up_factor.shape
    part_rank = rank // mp_count
    part_cols = out_width // mp_count
    rows = hidden_input.shape[0]
    own_blocks = tenant_of_block.shape[0] // dp_count
    block_rows = rows // own_blocks

    near = math.gcd(4, dp_count)
    team = group_count * near
    features = half_width // team
    teams = [
        [(gi * dp_count + base + k) * mp_count + mi for gi in range(group_count) for k in range(near)]
        for base in range(0, dp_count, near)
        for mi in range(mp_count)
    ]

    def swap(value, axis, bit):
        size = lax.axis_size(axis)
        return lax.ppermute(value, axis, [(k, k ^ bit) for k in range(size)])

    def shape(*dims):
        return jax.ShapeDtypeStruct(dims, bf16)

    def call(kernel, name, outs, in_specs, *values, scratch=(), out_specs=VMEM, params=PARAMS):
        return pl.pallas_call(
            kernel, in_specs=in_specs, out_specs=out_specs, out_shape=outs, scratch_shapes=list(scratch),
            compiler_params=params, name=name,
        )(*values)

    dp_bits = [1 << k for k in range(dp_count.bit_length() - 1)]
    near_bits = [bit for bit in dp_bits if bit < near]
    tie = lax.optimization_barrier

    repeats = dp_count // near
    leaving = [[k for k in range(dp_count) if k & 1 and bool(k & 2) == sooner] for sooner in (True, False)]
    remaining = [k for k in range(dp_count) if not k & 1]
    weighted, my_cols, *picked, block = call(
        functools.partial(prepare_kernel, leaving), "prepare",
        [
            shape(rows, out_width),
            shape(rows, part_cols),
            shape(len(leaving[0]), own_blocks, part_rank, out_width),
            shape(len(leaving[1]), own_blocks, part_rank, out_width),
            shape(1, own_blocks, part_rank, out_width),
        ],
        [HBM] * 6, rollout_row_counts[None], upstream, tenant_of_block, adapter_up_factor, common_down_factor.T,
        hidden_input, out_specs=[VMEM] * 5, params=pltpu.CompilerParams(),
        scratch=[
            pltpu.VMEM((1, rows), jnp.int32),
            pltpu.VMEM((rows, out_width), bf16),
            pltpu.SMEM(tenant_of_block.shape, jnp.int32),
            pltpu.VMEM(adapter_up_factor.shape, bf16),
            pltpu.VMEM((part_rank, common_down_factor.shape[0]), bf16),
            pltpu.VMEM(hidden_input.shape, bf16),
            pltpu.SemaphoreType.DMA((6,)),
        ],
    )
    to_send = call(
        spread_kernel, "spread", shape(repeats, near * features, cols), [HBM] * 2, frozen_value_weight, block,
        out_specs=HBM, params=pltpu.CompilerParams(),
        scratch=[
            pltpu.VMEM((near * features, cols), bf16),
            pltpu.SemaphoreType.DMA((4,)),
            pltpu.SemaphoreType.DMA((repeats, 4)),
        ],
    )
    row_steps = [("dp", bit, bit) for bit in near_bits[1:] + near_bits[:1]] + [
        ("groups", 1 << k, near << k) for k in range(group_count.bit_length() - 1)
    ]
    team_rows, distances = my_cols[None], [0]
    held = [[k ^ 1 for k in ks] for ks in leaving]
    got = [swap(value, "dp", 1) for value in picked]

    def useful(keys):
        return [i for i, kept in enumerate(held) if set(kept) & set(keys)]
    pieces, orders = [block], [[0]]
    last = []

    def up_step(bit):
        leaving = [k for k in remaining if k & bit]
        some = useful(leaving)
        value = call(
            functools.partial(pick_kernel, leaving, [held[i] for i in some]), "pick",
            shape(len(leaving), own_blocks, part_rank, out_width), [SMEM, VMEM] + [VMEM] * len(some),
            tenant_of_block, adapter_up_factor, *[got[i] for i in some],
        )
        last.append(value)
        remaining[:] = [k for k in remaining if not k & bit]
        held.append(list(remaining))
        got.append(swap(value, "dp", bit))

    def gathered():
        return [k for order in orders for k in order if k is not None]

    def block_step(bit):
        kept = [value[order.count(None) :] for value, order in zip(pieces, orders)]
        value = jnp.concatenate(kept) if len(kept) > 1 else kept[0]
        last.append(value)
        orders.append([k | bit for k in gathered()])
        pieces.append(swap(value, "dp", bit))

    def both_step(bit):
        leaving = [k for k in remaining if k & bit]
        blocks = gathered()
        some = useful(leaving)
        value = call(
            functools.partial(both_kernel, leaving, [held[i] for i in some]), "both",
            shape(len(leaving) + len(blocks), own_blocks, part_rank, out_width),
            [SMEM, VMEM] + [VMEM] * (len(some) + len(pieces)),
            tenant_of_block, adapter_up_factor, *[got[i] for i in some], *pieces,
        )
        last.append(value)
        remaining[:] = [k for k in remaining if not k & bit]
        arrived = swap(value, "dp", bit)
        held.append(list(remaining))
        got.append(arrived)
        orders.append([None] * len(leaving) + [k | bit for k in blocks])
        pieces.append(arrived)

    up_bits, block_bits = dp_bits[1:], dp_bits[::-1]
    for step, (axis, bit, distance) in enumerate(row_steps):
        new_rows = swap(team_rows, axis, bit)
        if step == 1 and up_bits[0] == block_bits[0]:
            both_step(up_bits.pop(0))
            block_bits.pop(0)
        else:
            if step:
                up_step(up_bits.pop(0))
            block_step(block_bits.pop(0))
        if step == 1:
            to_send, *_ = tie((to_send, team_rows, *last))
        if step == 0:
            team_rows, new_rows, got[:1], to_send = tie((team_rows, new_rows, got[:1], to_send))
        elif step < len(row_steps) - 1:
            team_rows, new_rows, got[::2], pieces = tie((team_rows, new_rows, got[::2], pieces))
        else:
            new_rows, got[1] = tie((new_rows, got[1]))
        team_rows = jnp.concatenate([team_rows, new_rows])
        distances = distances + [k | distance for k in distances]
    other_rows = swap(team_rows, "mp", 1)
    weight_slices = lax.all_to_all(
        to_send.reshape(dp_count, features, cols), "dp", split_axis=0, concat_axis=0, tiled=True
    )

    weight_slices, _ = tie((weight_slices, last))
    if cols % 128:
        slices = weight_slices.transpose(1, 0, 2).reshape(features, 2, part_cols).transpose(1, 0, 2)
    else:
        slices = weight_slices
    frozen = call(
        functools.partial(frozen_kernel, near, distances), "frozen", shape(team, rows, features), [VMEM, VMEM, VMEM],
        team_rows, other_rows, slices, out_specs=HBM,
        scratch=[
            pltpu.VMEM((2, features, part_cols), bf16),
            pltpu.VMEM((team, rows, features), bf16),
            pltpu.SemaphoreType.DMA((team,)),
        ],
    )
    frozen, got, pieces = tie((frozen, got, pieces))
    frozen_mine = lax.all_to_all(
        frozen, ALL, split_axis=0, concat_axis=0, tiled=True, axis_index_groups=teams
    )
    for bit in up_bits:
        up_step(bit)
    for bit in block_bits:
        block_step(bit)
    some = useful([0])
    back_part = call(
        functools.partial(back_kernel, [held[i] for i in some]), "back", shape(part_rank, rows),
        [SMEM, VMEM, VMEM] + [VMEM] * len(some), tenant_of_block, adapter_up_factor, weighted, *[got[i] for i in some],
    )

    grad_part = call(
        functools.partial(gradient_kernel, orders, adapter_scale / block_rows), "gradient",
        shape(tenants_here, part_rank, out_width), [SMEM] + [VMEM] * len(pieces), tenant_of_block, *pieces,
    )
    input_gradient, up_factor_gradient = call(
        last_kernel, "last", [shape(rows, half_width), shape(*adapter_up_factor.shape)], [VMEM] * 6,
        frozen_mine, back_part, swap(back_part, "mp", 1), common_down_factor.T, grad_part, swap(grad_part, "mp", 1),
        out_specs=[HBM, HBM],
        scratch=[
            pltpu.VMEM((rank, rows), bf16),
            pltpu.VMEM((team, rows, features), bf16),
            pltpu.SemaphoreType.DMA((team,)),
            pltpu.SemaphoreType.DMA((2,)),
        ],
    )
    return (input_gradient, up_factor_gradient)


def solution(mesh):
    placed = (
        P(("groups", "dp"), None),
        P(("groups", "dp"), None),
        P(("groups", "dp")),
        P("groups"),
        P("mp", "dp"),
        P(),
        P(("groups", "dp"), None, None),
    )
    return jax.shard_map(
        local,
        mesh=mesh,
        in_specs=placed,
        out_specs=(P(("groups", "dp"), "mp"), P(("groups", "dp"), None, None)),
        check_vma=False,
    )
```

```python
import functools
import math

import jax
import jax.numpy as jnp
from jax import lax
from jax.experimental import pallas as pl
from jax.experimental.pallas import tpu as pltpu
from jax.sharding import PartitionSpec as P

adapter_scale = 2.0
ALL = ("groups", "dp", "mp")
f32, bf16 = jnp.float32, jnp.bfloat16
VMEM = pl.BlockSpec(memory_space=pltpu.VMEM)
SMEM = pl.BlockSpec(memory_space=pltpu.SMEM)
HBM = pl.BlockSpec(memory_space=pltpu.HBM)
PARAMS = pltpu.CompilerParams(vmem_limit_bytes=16 * 1024 * 1024)


def place():
    return lax.axis_index("groups"), lax.axis_index("dp"), lax.axis_index("mp")


def piece(index, size):
    return pl.ds(pl.multiple_of(index * size, size), size)


def prepare_kernel(
    leaving, counts, upstream, tenants, up, down, hidden, weighted, my_cols, sooner, later, block,
    held_counts, held_upstream, held_tenants, held_up, held_down, held_hidden, sem,
):
    _, _, m = place()
    _, own_blocks, part_rank, _ = block.shape
    loads = [
        pltpu.make_async_copy(source, target, sem.at[i])
        for i, (source, target) in enumerate(
            [
                (counts, held_counts),
                (upstream, held_upstream),
                (tenants, held_tenants),
                (up, held_up),
                (down.at[piece(m, part_rank)], held_down),
                (hidden, held_hidden),
            ]
        )
    ]
    for load in loads:
        load.start()
    rows, part = my_cols.shape
    diagonal = lax.broadcasted_iota(jnp.int32, (rows, rows), 0) == lax.broadcasted_iota(jnp.int32, (rows, rows), 1)
    loads[0].wait()
    scale = jnp.where(diagonal, held_counts[...].astype(f32), 0.0).astype(bf16)
    loads[1].wait()
    weighted[...] = jnp.dot(scale, held_upstream[...], preferred_element_type=f32).astype(bf16)
    my_cols[...] = weighted[:, piece(m, part)]
    loads[2].wait()
    loads[3].wait()
    for ks, picked in zip(leaving, (sooner, later)):
        for i, k in enumerate(ks):
            for n in range(own_blocks):
                picked[i, n] = chosen(held_tenants, held_up, k, n, own_blocks, part_rank)
    loads[4].wait()
    loads[5].wait()
    low = lax.dot_general(
        held_down[...], held_hidden[...], (((1,), (1,)), ((), ())), preferred_element_type=f32
    ).astype(bf16)
    size = rows // own_blocks
    for n in range(own_blocks):
        at = slice(n * size, (n + 1) * size)
        block[0, n] = jnp.dot(low[:, at], weighted[at], preferred_element_type=f32).astype(bf16)


def spread_kernel(weight, _, to_send, held, in_sem, out_sem):
    g, _, _ = place()
    copies, depth = to_send.shape[0], to_send.shape[1]
    chunks = in_sem.shape[0]
    size = depth // chunks
    loads, stores = [], []
    for c in range(chunks):
        at = pl.ds(pl.multiple_of(g * depth + c * size, size), size)
        loads.append(pltpu.make_async_copy(weight.at[at], held.at[pl.ds(c * size, size)], in_sem.at[c]))
        loads[-1].start()
    for c in range(chunks):
        loads[c].wait()
        for k in range(copies):
            at = pl.ds(c * size, size)
            stores.append(pltpu.make_async_copy(held.at[at], to_send.at[k, at], out_sem.at[k, c]))
            stores[-1].start()
    for store in stores:
        store.wait()


def chosen(tenants, up, distance, n, own_blocks, part_rank):
    _, d, m = place()
    wanted = tenants[(d ^ distance) * own_blocks + n] - d * up.shape[0]
    total = jnp.zeros((part_rank, up.shape[2]), bf16)
    for t in range(up.shape[0]):
        total = jnp.where(wanted == t, up[t, piece(m, part_rank)], total)
    return total


def pick_kernel(leaving, held, tenants, up, *refs):
    out = refs[-1]
    for i, k in enumerate(leaving):
        for n in range(out.shape[1]):
            value = chosen(tenants, up, k, n, out.shape[1], out.shape[2])
            for kept, got in zip(held, refs[:-1]):
                if k in kept:
                    value = value + got[kept.index(k), n]
            out[i, n] = value


def both_kernel(leaving, held, tenants, up, *refs):
    out = refs[-1]
    pick_kernel(leaving, held, tenants, up, *refs[: len(held)], out.at[: len(leaving)])
    at = len(leaving)
    for blocks in refs[len(held) : -1]:
        out[at : at + blocks.shape[0]] = blocks[...]
        at += blocks.shape[0]


def back_kernel(held, tenants, up, weighted, *refs):
    out = refs[-1]
    part_rank, rows = out.shape
    own_blocks = refs[0].shape[1]
    size = rows // own_blocks
    for n in range(own_blocks):
        value = chosen(tenants, up, 0, n, own_blocks, part_rank)
        for kept, got in zip(held, refs[:-1]):
            if 0 in kept:
                value = value + got[kept.index(0), n]
        at = slice(n * size, (n + 1) * size)
        out[:, at] = lax.dot_general(
            value, weighted[at], (((1,), (1,)), ((), ())), preferred_element_type=f32
        ).astype(bf16)


def gradient_kernel(orders, scale, tenants, *refs):
    out = refs[-1]
    _, d, _ = place()
    for t in range(out.shape[0]):
        total = jnp.zeros(out.shape[1:], f32)
        for order, got in zip(orders, refs[:-1]):
            own_blocks = got.shape[1]
            for i, k in enumerate(order):
                for n in range(own_blocks if k is not None else 0):
                    wanted = tenants[(d ^ k) * own_blocks + n] - d * out.shape[0]
                    total = total + jnp.where(wanted == t, got[i, n].astype(f32), 0.0)
        out[t] = (total * scale).astype(bf16)


def frozen_kernel(near, distances, mine, other, slices, out, held, ready, sem):
    team, rows, part = mine.shape
    count, features, width = slices.shape
    per_part = count // 2
    g, d, m = place()
    own = g * near + lax.rem(d, near)
    for half in range(2):
        at = lax.rem(m + half, 2) * per_part
        for j in range(per_part):
            held[half, :, j * width : (j + 1) * width] = slices[at + j]
    dims = (((1,), (1,)), ((), ()))
    stores = []
    for c in range(0, team, 2):
        total = lax.dot_general(mine[c : c + 2].reshape(2 * rows, part), held[0], dims, preferred_element_type=f32)
        total += lax.dot_general(other[c : c + 2].reshape(2 * rows, part), held[1], dims, preferred_element_type=f32)
        ready[c : c + 2] = total.astype(bf16).reshape(2, rows, features)
        for k in range(c, c + 2):
            stores.append(pltpu.make_async_copy(ready.at[k], out.at[own ^ distances[k]], sem.at[k]))
            stores[-1].start()
    for store in stores:
        store.wait()


def last_kernel(frozen, mine, other, down, gradient, other_gradient, out, whole, back, held, sem, gradient_sem):
    team, rows, features = frozen.shape
    part_rank, _ = mine.shape
    _, _, m = place()
    stores = [
        pltpu.make_async_copy(gradient, whole.at[:, piece(m, part_rank)], gradient_sem.at[0]),
        pltpu.make_async_copy(other_gradient, whole.at[:, piece(1 - m, part_rank)], gradient_sem.at[1]),
    ]
    for store in stores:
        store.start()
    back[piece(m, part_rank)] = mine[...]
    back[piece(1 - m, part_rank)] = other[...]
    for k in range(team):
        at = pl.ds(pl.multiple_of(m * (team * features) + k * features, features), features)
        adapter = lax.dot_general(back[...], down[:, at], (((0,), (0,)), ((), ())), preferred_element_type=f32)
        held[k] = (frozen[k].astype(f32) + adapter_scale * adapter).astype(bf16)
        stores.append(pltpu.make_async_copy(held.at[k], out.at[:, pl.ds(k * features, features)], sem.at[k]))
        stores[-1].start()
    for store in stores:
        store.wait()


def local(
    hidden_input,
    upstream,
    rollout_row_counts,
    tenant_of_block,
    frozen_value_weight,
    common_down_factor,
    adapter_up_factor,
):
    group_count = lax.axis_size("groups")
    dp_count = lax.axis_size("dp")
    mp_count = lax.axis_size("mp")
    half_width, cols = frozen_value_weight.shape
    tenants_here, rank, out_width = adapter_up_factor.shape
    part_rank = rank // mp_count
    part_cols = out_width // mp_count
    rows = hidden_input.shape[0]
    own_blocks = tenant_of_block.shape[0] // dp_count
    block_rows = rows // own_blocks

    near = math.gcd(4, dp_count)
    team = group_count * near
    features = half_width // team
    teams = [
        [(gi * dp_count + base + k) * mp_count + mi for gi in range(group_count) for k in range(near)]
        for base in range(0, dp_count, near)
        for mi in range(mp_count)
    ]

    def swap(value, axis, bit):
        size = lax.axis_size(axis)
        return lax.ppermute(value, axis, [(k, k ^ bit) for k in range(size)])

    def shape(*dims):
        return jax.ShapeDtypeStruct(dims, bf16)

    def call(kernel, name, outs, in_specs, *values, scratch=(), out_specs=VMEM, params=PARAMS):
        return pl.pallas_call(
            kernel, in_specs=in_specs, out_specs=out_specs, out_shape=outs, scratch_shapes=list(scratch),
            compiler_params=params, name=name,
        )(*values)

    dp_bits = [1 << k for k in range(dp_count.bit_length() - 1)]
    near_bits = [bit for bit in dp_bits if bit < near]
    tie = lax.optimization_barrier

    repeats = dp_count // near
    leaving = [[k for k in range(dp_count) if k & 1 and bool(k & 2) == sooner] for sooner in (True, False)]
    remaining = [k for k in range(dp_count) if not k & 1]
    weighted, my_cols, *picked, block = call(
        functools.partial(prepare_kernel, leaving), "prepare",
        [
            shape(rows, out_width),
            shape(rows, part_cols),
            shape(len(leaving[0]), own_blocks, part_rank, out_width),
            shape(len(leaving[1]), own_blocks, part_rank, out_width),
            shape(1, own_blocks, part_rank, out_width),
        ],
        [HBM] * 6, rollout_row_counts[None], upstream, tenant_of_block, adapter_up_factor, common_down_factor.T,
        hidden_input, out_specs=[VMEM] * 5, params=pltpu.CompilerParams(),
        scratch=[
            pltpu.VMEM((1, rows), jnp.int32),
            pltpu.VMEM((rows, out_width), bf16),
            pltpu.SMEM(tenant_of_block.shape, jnp.int32),
            pltpu.VMEM(adapter_up_factor.shape, bf16),
            pltpu.VMEM((part_rank, common_down_factor.shape[0]), bf16),
            pltpu.VMEM(hidden_input.shape, bf16),
            pltpu.SemaphoreType.DMA((6,)),
        ],
    )
    to_send = call(
        spread_kernel, "spread", shape(repeats, near * features, cols), [HBM] * 2, frozen_value_weight, block,
        out_specs=HBM, params=pltpu.CompilerParams(),
        scratch=[
            pltpu.VMEM((near * features, cols), bf16),
            pltpu.SemaphoreType.DMA((4,)),
            pltpu.SemaphoreType.DMA((repeats, 4)),
        ],
    )
    row_steps = [("dp", bit, bit) for bit in near_bits[1:] + near_bits[:1]] + [
        ("groups", 1 << k, near << k) for k in range(group_count.bit_length() - 1)
    ]
    team_rows, distances = my_cols[None], [0]
    held = [[k ^ 1 for k in ks] for ks in leaving]
    got = [swap(value, "dp", 1) for value in picked]

    def useful(keys):
        return [i for i, kept in enumerate(held) if set(kept) & set(keys)]
    pieces, orders = [block], [[0]]
    last = []

    def up_step(bit):
        leaving = [k for k in remaining if k & bit]
        some = useful(leaving)
        value = call(
            functools.partial(pick_kernel, leaving, [held[i] for i in some]), "pick",
            shape(len(leaving), own_blocks, part_rank, out_width), [SMEM, VMEM] + [VMEM] * len(some),
            tenant_of_block, adapter_up_factor, *[got[i] for i in some],
        )
        last.append(value)
        remaining[:] = [k for k in remaining if not k & bit]
        held.append(list(remaining))
        got.append(swap(value, "dp", bit))

    def gathered():
        return [k for order in orders for k in order if k is not None]

    def block_step(bit):
        kept = [value[order.count(None) :] for value, order in zip(pieces, orders)]
        value = jnp.concatenate(kept) if len(kept) > 1 else kept[0]
        last.append(value)
        orders.append([k | bit for k in gathered()])
        pieces.append(swap(value, "dp", bit))

    def both_step(bit):
        leaving = [k for k in remaining if k & bit]
        blocks = gathered()
        some = useful(leaving)
        value = call(
            functools.partial(both_kernel, leaving, [held[i] for i in some]), "both",
            shape(len(leaving) + len(blocks), own_blocks, part_rank, out_width),
            [SMEM, VMEM] + [VMEM] * (len(some) + len(pieces)),
            tenant_of_block, adapter_up_factor, *[got[i] for i in some], *pieces,
        )
        last.append(value)
        remaining[:] = [k for k in remaining if not k & bit]
        arrived = swap(value, "dp", bit)
        held.append(list(remaining))
        got.append(arrived)
        orders.append([None] * len(leaving) + [k | bit for k in blocks])
        pieces.append(arrived)

    up_bits, block_bits = dp_bits[1:], dp_bits[::-1]
    for step, (axis, bit, distance) in enumerate(row_steps):
        new_rows = swap(team_rows, axis, bit)
        if step == 1 and up_bits[0] == block_bits[0]:
            both_step(up_bits.pop(0))
            block_bits.pop(0)
        else:
            if step:
                up_step(up_bits.pop(0))
            block_step(block_bits.pop(0))
        if step == 1:
            to_send, *_ = tie((to_send, team_rows, *last))
        if step == 0:
            team_rows, new_rows, got[:1], to_send = tie((team_rows, new_rows, got[:1], to_send))
        elif step < len(row_steps) - 1:
            team_rows, new_rows, got[::2], pieces = tie((team_rows, new_rows, got[::2], pieces))
        else:
            new_rows, got[1] = tie((new_rows, got[1]))
        team_rows = jnp.concatenate([team_rows, new_rows])
        distances = distances + [k | distance for k in distances]
    other_rows = swap(team_rows, "mp", 1)
    weight_slices = lax.all_to_all(
        to_send.reshape(dp_count, features, cols), "dp", split_axis=0, concat_axis=0, tiled=True
    )

    weight_slices, _ = tie((weight_slices, last))
    if cols % 128:
        slices = weight_slices.transpose(1, 0, 2).reshape(features, 2, part_cols).transpose(1, 0, 2)
    else:
        slices = weight_slices
    frozen = call(
        functools.partial(frozen_kernel, near, distances), "frozen", shape(team, rows, features), [VMEM, VMEM, VMEM],
        team_rows, other_rows, slices, out_specs=HBM,
        scratch=[
            pltpu.VMEM((2, features, part_cols), bf16),
            pltpu.VMEM((team, rows, features), bf16),
            pltpu.SemaphoreType.DMA((team,)),
        ],
    )
    frozen, *_ = tie((frozen, got, pieces))
    frozen_mine = lax.all_to_all(
        frozen, ALL, split_axis=0, concat_axis=0, tiled=True, axis_index_groups=teams
    )
    for bit in up_bits:
        up_step(bit)
    for bit in block_bits:
        block_step(bit)
    some = useful([0])
    back_part = call(
        functools.partial(back_kernel, [held[i] for i in some]), "back", shape(part_rank, rows),
        [SMEM, VMEM, VMEM] + [VMEM] * len(some), tenant_of_block, adapter_up_factor, weighted, *[got[i] for i in some],
    )

    grad_part = call(
        functools.partial(gradient_kernel, orders, adapter_scale / block_rows), "gradient",
        shape(tenants_here, part_rank, out_width), [SMEM] + [VMEM] * len(pieces), tenant_of_block, *pieces,
    )
    input_gradient, up_factor_gradient = call(
        last_kernel, "last", [shape(rows, half_width), shape(*adapter_up_factor.shape)], [VMEM] * 6,
        frozen_mine, back_part, swap(back_part, "mp", 1), common_down_factor.T, grad_part, swap(grad_part, "mp", 1),
        out_specs=[HBM, HBM],
        scratch=[
            pltpu.VMEM((rank, rows), bf16),
            pltpu.VMEM((team, rows, features), bf16),
            pltpu.SemaphoreType.DMA((team,)),
            pltpu.SemaphoreType.DMA((2,)),
        ],
    )
    return (input_gradient, up_factor_gradient)


def solution(mesh):
    placed = (
        P(("groups", "dp"), None),
        P(("groups", "dp"), None),
        P(("groups", "dp")),
        P("groups"),
        P("mp", "dp"),
        P(),
        P(("groups", "dp"), None, None),
    )
    return jax.shard_map(
        local,
        mesh=mesh,
        in_specs=placed,
        out_specs=(P(("groups", "dp"), "mp"), P(("groups", "dp"), None, None)),
        check_vma=False,
    )
```

```python
import functools
import math

import jax
import jax.numpy as jnp
from jax import lax
from jax.experimental import pallas as pl
from jax.experimental.pallas import tpu as pltpu
from jax.sharding import PartitionSpec as P

adapter_scale = 2.0
ALL = ("groups", "dp", "mp")
f32, bf16 = jnp.float32, jnp.bfloat16
VMEM = pl.BlockSpec(memory_space=pltpu.VMEM)
SMEM = pl.BlockSpec(memory_space=pltpu.SMEM)
HBM = pl.BlockSpec(memory_space=pltpu.HBM)
PARAMS = pltpu.CompilerParams(vmem_limit_bytes=16 * 1024 * 1024)


def place():
    return lax.axis_index("groups"), lax.axis_index("dp"), lax.axis_index("mp")


def piece(index, size):
    return pl.ds(pl.multiple_of(index * size, size), size)


def prepare_kernel(
    leaving, counts, upstream, tenants, up, down, hidden, weighted, my_cols, sooner, later, block,
    held_counts, held_upstream, held_tenants, held_up, held_down, held_hidden, sem,
):
    _, _, m = place()
    _, own_blocks, part_rank, _ = block.shape
    loads = [
        pltpu.make_async_copy(source, target, sem.at[i])
        for i, (source, target) in enumerate(
            [
                (counts, held_counts),
                (upstream, held_upstream),
                (tenants, held_tenants),
                (up, held_up),
                (down.at[piece(m, part_rank)], held_down),
                (hidden, held_hidden),
            ]
        )
    ]
    for load in loads[:2] + loads[5:] + loads[2:5]:
        load.start()
    rows, part = my_cols.shape
    diagonal = lax.broadcasted_iota(jnp.int32, (rows, rows), 0) == lax.broadcasted_iota(jnp.int32, (rows, rows), 1)
    loads[0].wait()
    scale = jnp.where(diagonal, held_counts[...].astype(f32), 0.0).astype(bf16)
    loads[1].wait()
    weighted[...] = jnp.dot(scale, held_upstream[...], preferred_element_type=f32).astype(bf16)
    my_cols[...] = weighted[:, piece(m, part)]
    loads[2].wait()
    loads[3].wait()
    for ks, picked in zip(leaving, (sooner, later)):
        for i, k in enumerate(ks):
            for n in range(own_blocks):
                picked[i, n] = chosen(held_tenants, held_up, k, n, own_blocks, part_rank)
    loads[4].wait()
    loads[5].wait()
    low = lax.dot_general(
        held_down[...], held_hidden[...], (((1,), (1,)), ((), ())), preferred_element_type=f32
    ).astype(bf16)
    size = rows // own_blocks
    for n in range(own_blocks):
        at = slice(n * size, (n + 1) * size)
        block[0, n] = jnp.dot(low[:, at], weighted[at], preferred_element_type=f32).astype(bf16)


def spread_kernel(weight, _, to_send, held, in_sem, out_sem):
    g, _, _ = place()
    copies, depth = to_send.shape[0], to_send.shape[1]
    chunks = in_sem.shape[0]
    size = depth // chunks
    loads, stores = [], []
    for c in range(chunks):
        at = pl.ds(pl.multiple_of(g * depth + c * size, size), size)
        loads.append(pltpu.make_async_copy(weight.at[at], held.at[pl.ds(c * size, size)], in_sem.at[c]))
        loads[-1].start()
    for c in range(chunks):
        loads[c].wait()
        for k in range(copies):
            at = pl.ds(c * size, size)
            stores.append(pltpu.make_async_copy(held.at[at], to_send.at[k, at], out_sem.at[k, c]))
            stores[-1].start()
    for store in stores:
        store.wait()


def chosen(tenants, up, distance, n, own_blocks, part_rank):
    _, d, m = place()
    wanted = tenants[(d ^ distance) * own_blocks + n] - d * up.shape[0]
    total = jnp.zeros((part_rank, up.shape[2]), bf16)
    for t in range(up.shape[0]):
        total = jnp.where(wanted == t, up[t, piece(m, part_rank)], total)
    return total


def pick_kernel(leaving, held, tenants, up, *refs):
    out = refs[-1]
    for i, k in enumerate(leaving):
        for n in range(out.shape[1]):
            value = chosen(tenants, up, k, n, out.shape[1], out.shape[2])
            for kept, got in zip(held, refs[:-1]):
                if k in kept:
                    value = value + got[kept.index(k), n]
            out[i, n] = value


def both_kernel(leaving, held, tenants, up, *refs):
    out = refs[-1]
    pick_kernel(leaving, held, tenants, up, *refs[: len(held)], out.at[: len(leaving)])
    at = len(leaving)
    for blocks in refs[len(held) : -1]:
        out[at : at + blocks.shape[0]] = blocks[...]
        at += blocks.shape[0]


def back_kernel(held, tenants, up, weighted, *refs):
    out = refs[-1]
    part_rank, rows = out.shape
    own_blocks = refs[0].shape[1]
    size = rows // own_blocks
    for n in range(own_blocks):
        value = chosen(tenants, up, 0, n, own_blocks, part_rank)
        for kept, got in zip(held, refs[:-1]):
            if 0 in kept:
                value = value + got[kept.index(0), n]
        at = slice(n * size, (n + 1) * size)
        out[:, at] = lax.dot_general(
            value, weighted[at], (((1,), (1,)), ((), ())), preferred_element_type=f32
        ).astype(bf16)


def gradient_kernel(orders, scale, tenants, *refs):
    out = refs[-1]
    _, d, _ = place()
    for t in range(out.shape[0]):
        total = jnp.zeros(out.shape[1:], f32)
        for order, got in zip(orders, refs[:-1]):
            own_blocks = got.shape[1]
            for i, k in enumerate(order):
                for n in range(own_blocks if k is not None else 0):
                    wanted = tenants[(d ^ k) * own_blocks + n] - d * out.shape[0]
                    total = total + jnp.where(wanted == t, got[i, n].astype(f32), 0.0)
        out[t] = (total * scale).astype(bf16)


def frozen_kernel(near, distances, mine, other, slices, out, held, ready, sem):
    team, rows, part = mine.shape
    count, features, width = slices.shape
    per_part = count // 2
    g, d, m = place()
    own = g * near + lax.rem(d, near)
    for half in range(2):
        at = lax.rem(m + half, 2) * per_part
        for j in range(per_part):
            held[half, :, j * width : (j + 1) * width] = slices[at + j]
    dims = (((1,), (1,)), ((), ()))
    stores = []
    for c in range(0, team, 2):
        total = lax.dot_general(mine[c : c + 2].reshape(2 * rows, part), held[0], dims, preferred_element_type=f32)
        total += lax.dot_general(other[c : c + 2].reshape(2 * rows, part), held[1], dims, preferred_element_type=f32)
        ready[c : c + 2] = total.astype(bf16).reshape(2, rows, features)
        for k in range(c, c + 2):
            stores.append(pltpu.make_async_copy(ready.at[k], out.at[own ^ distances[k]], sem.at[k]))
            stores[-1].start()
    for store in stores:
        store.wait()


def last_kernel(frozen, mine, other, down, gradient, other_gradient, out, whole, back, held, sem, gradient_sem):
    team, rows, features = frozen.shape
    part_rank, _ = mine.shape
    _, _, m = place()
    stores = [
        pltpu.make_async_copy(gradient, whole.at[:, piece(m, part_rank)], gradient_sem.at[0]),
        pltpu.make_async_copy(other_gradient, whole.at[:, piece(1 - m, part_rank)], gradient_sem.at[1]),
    ]
    for store in stores:
        store.start()
    back[piece(m, part_rank)] = mine[...]
    back[piece(1 - m, part_rank)] = other[...]
    for k in range(team):
        at = pl.ds(pl.multiple_of(m * (team * features) + k * features, features), features)
        adapter = lax.dot_general(back[...], down[:, at], (((0,), (0,)), ((), ())), preferred_element_type=f32)
        held[k] = (frozen[k].astype(f32) + adapter_scale * adapter).astype(bf16)
        stores.append(pltpu.make_async_copy(held.at[k], out.at[:, pl.ds(k * features, features)], sem.at[k]))
        stores[-1].start()
    for store in stores:
        store.wait()


def local(
    hidden_input,
    upstream,
    rollout_row_counts,
    tenant_of_block,
    frozen_value_weight,
    common_down_factor,
    adapter_up_factor,
):
    group_count = lax.axis_size("groups")
    dp_count = lax.axis_size("dp")
    mp_count = lax.axis_size("mp")
    half_width, cols = frozen_value_weight.shape
    tenants_here, rank, out_width = adapter_up_factor.shape
    part_rank = rank // mp_count
    part_cols = out_width // mp_count
    rows = hidden_input.shape[0]
    own_blocks = tenant_of_block.shape[0] // dp_count
    block_rows = rows // own_blocks

    near = math.gcd(4, dp_count)
    team = group_count * near
    features = half_width // team
    teams = [
        [(gi * dp_count + base + k) * mp_count + mi for gi in range(group_count) for k in range(near)]
        for base in range(0, dp_count, near)
        for mi in range(mp_count)
    ]

    def swap(value, axis, bit):
        size = lax.axis_size(axis)
        return lax.ppermute(value, axis, [(k, k ^ bit) for k in range(size)])

    def shape(*dims):
        return jax.ShapeDtypeStruct(dims, bf16)

    def call(kernel, name, outs, in_specs, *values, scratch=(), out_specs=VMEM, params=PARAMS):
        return pl.pallas_call(
            kernel, in_specs=in_specs, out_specs=out_specs, out_shape=outs, scratch_shapes=list(scratch),
            compiler_params=params, name=name,
        )(*values)

    dp_bits = [1 << k for k in range(dp_count.bit_length() - 1)]
    near_bits = [bit for bit in dp_bits if bit < near]
    tie = lax.optimization_barrier

    repeats = dp_count // near
    leaving = [[k for k in range(dp_count) if k & 1 and bool(k & 2) == sooner] for sooner in (True, False)]
    remaining = [k for k in range(dp_count) if not k & 1]
    weighted, my_cols, *picked, block = call(
        functools.partial(prepare_kernel, leaving), "prepare",
        [
            shape(rows, out_width),
            shape(rows, part_cols),
            shape(len(leaving[0]), own_blocks, part_rank, out_width),
            shape(len(leaving[1]), own_blocks, part_rank, out_width),
            shape(1, own_blocks, part_rank, out_width),
        ],
        [HBM] * 6, rollout_row_counts[None], upstream, tenant_of_block, adapter_up_factor, common_down_factor.T,
        hidden_input, out_specs=[VMEM] * 5, params=pltpu.CompilerParams(),
        scratch=[
            pltpu.VMEM((1, rows), jnp.int32),
            pltpu.VMEM((rows, out_width), bf16),
            pltpu.SMEM(tenant_of_block.shape, jnp.int32),
            pltpu.VMEM(adapter_up_factor.shape, bf16),
            pltpu.VMEM((part_rank, common_down_factor.shape[0]), bf16),
            pltpu.VMEM(hidden_input.shape, bf16),
            pltpu.SemaphoreType.DMA((6,)),
        ],
    )
    to_send = call(
        spread_kernel, "spread", shape(repeats, near * features, cols), [HBM] * 2, frozen_value_weight, block,
        out_specs=HBM, params=pltpu.CompilerParams(),
        scratch=[
            pltpu.VMEM((near * features, cols), bf16),
            pltpu.SemaphoreType.DMA((4,)),
            pltpu.SemaphoreType.DMA((repeats, 4)),
        ],
    )
    row_steps = [("dp", bit, bit) for bit in near_bits[1:] + near_bits[:1]] + [
        ("groups", 1 << k, near << k) for k in range(group_count.bit_length() - 1)
    ]
    team_rows, distances = my_cols[None], [0]
    held = [[k ^ 1 for k in ks] for ks in leaving]
    got = [swap(value, "dp", 1) for value in picked]

    def useful(keys):
        return [i for i, kept in enumerate(held) if set(kept) & set(keys)]
    pieces, orders = [block], [[0]]
    last = []

    def up_step(bit):
        leaving = [k for k in remaining if k & bit]
        some = useful(leaving)
        value = call(
            functools.partial(pick_kernel, leaving, [held[i] for i in some]), "pick",
            shape(len(leaving), own_blocks, part_rank, out_width), [SMEM, VMEM] + [VMEM] * len(some),
            tenant_of_block, adapter_up_factor, *[got[i] for i in some],
        )
        last.append(value)
        remaining[:] = [k for k in remaining if not k & bit]
        held.append(list(remaining))
        got.append(swap(value, "dp", bit))

    def gathered():
        return [k for order in orders for k in order if k is not None]

    def block_step(bit):
        kept = [value[order.count(None) :] for value, order in zip(pieces, orders)]
        value = jnp.concatenate(kept) if len(kept) > 1 else kept[0]
        last.append(value)
        orders.append([k | bit for k in gathered()])
        pieces.append(swap(value, "dp", bit))

    def both_step(bit):
        leaving = [k for k in remaining if k & bit]
        blocks = gathered()
        some = useful(leaving)
        value = call(
            functools.partial(both_kernel, leaving, [held[i] for i in some]), "both",
            shape(len(leaving) + len(blocks), own_blocks, part_rank, out_width),
            [SMEM, VMEM] + [VMEM] * (len(some) + len(pieces)),
            tenant_of_block, adapter_up_factor, *[got[i] for i in some], *pieces,
        )
        last.append(value)
        remaining[:] = [k for k in remaining if not k & bit]
        arrived = swap(value, "dp", bit)
        held.append(list(remaining))
        got.append(arrived)
        orders.append([None] * len(leaving) + [k | bit for k in blocks])
        pieces.append(arrived)

    up_bits, block_bits = dp_bits[1:], dp_bits[::-1]
    for step, (axis, bit, distance) in enumerate(row_steps):
        new_rows = swap(team_rows, axis, bit)
        if step == 1 and up_bits[0] == block_bits[0]:
            both_step(up_bits.pop(0))
            block_bits.pop(0)
        else:
            if step:
                up_step(up_bits.pop(0))
            block_step(block_bits.pop(0))
        if step == 1:
            to_send, *_ = tie((to_send, team_rows, *last))
        if step == 0:
            team_rows, new_rows, got[:1], to_send = tie((team_rows, new_rows, got[:1], to_send))
        elif step < len(row_steps) - 1:
            team_rows, new_rows, *_ = tie((team_rows, new_rows, got[::2], pieces))
        else:
            new_rows, _ = tie((new_rows, got[1]))
        team_rows = jnp.concatenate([team_rows, new_rows])
        distances = distances + [k | distance for k in distances]
    other_rows = swap(team_rows, "mp", 1)
    weight_slices = lax.all_to_all(
        to_send.reshape(dp_count, features, cols), "dp", split_axis=0, concat_axis=0, tiled=True
    )

    weight_slices, _ = tie((weight_slices, last))
    if cols % 128:
        slices = weight_slices.transpose(1, 0, 2).reshape(features, 2, part_cols).transpose(1, 0, 2)
    else:
        slices = weight_slices
    frozen = call(
        functools.partial(frozen_kernel, near, distances), "frozen", shape(team, rows, features), [VMEM, VMEM, VMEM],
        team_rows, other_rows, slices, out_specs=HBM,
        scratch=[
            pltpu.VMEM((2, features, part_cols), bf16),
            pltpu.VMEM((team, rows, features), bf16),
            pltpu.SemaphoreType.DMA((team,)),
        ],
    )
    frozen, *_ = tie((frozen, got, pieces))
    frozen_mine = lax.all_to_all(
        frozen, ALL, split_axis=0, concat_axis=0, tiled=True, axis_index_groups=teams
    )
    for bit in up_bits:
        up_step(bit)
    for bit in block_bits:
        block_step(bit)
    some = useful([0])
    back_part = call(
        functools.partial(back_kernel, [held[i] for i in some]), "back", shape(part_rank, rows),
        [SMEM, VMEM, VMEM] + [VMEM] * len(some), tenant_of_block, adapter_up_factor, weighted, *[got[i] for i in some],
    )

    grad_part = call(
        functools.partial(gradient_kernel, orders, adapter_scale / block_rows), "gradient",
        shape(tenants_here, part_rank, out_width), [SMEM] + [VMEM] * len(pieces), tenant_of_block, *pieces,
    )
    input_gradient, up_factor_gradient = call(
        last_kernel, "last", [shape(rows, half_width), shape(*adapter_up_factor.shape)], [VMEM] * 6,
        frozen_mine, back_part, swap(back_part, "mp", 1), common_down_factor.T, grad_part, swap(grad_part, "mp", 1),
        out_specs=[HBM, HBM],
        scratch=[
            pltpu.VMEM((rank, rows), bf16),
            pltpu.VMEM((team, rows, features), bf16),
            pltpu.SemaphoreType.DMA((team,)),
            pltpu.SemaphoreType.DMA((2,)),
        ],
    )
    return (input_gradient, up_factor_gradient)


def solution(mesh):
    placed = (
        P(("groups", "dp"), None),
        P(("groups", "dp"), None),
        P(("groups", "dp")),
        P("groups"),
        P("mp", "dp"),
        P(),
        P(("groups", "dp"), None, None),
    )
    return jax.shard_map(
        local,
        mesh=mesh,
        in_specs=placed,
        out_specs=(P(("groups", "dp"), "mp"), P(("groups", "dp"), None, None)),
        check_vma=False,
    )
```

```python
import functools
import math

import jax
import jax.numpy as jnp
from jax import lax
from jax.experimental import pallas as pl
from jax.experimental.pallas import tpu as pltpu
from jax.sharding import PartitionSpec as P

adapter_scale = 2.0
ALL = ("groups", "dp", "mp")
f32, bf16 = jnp.float32, jnp.bfloat16
VMEM = pl.BlockSpec(memory_space=pltpu.VMEM)
SMEM = pl.BlockSpec(memory_space=pltpu.SMEM)
HBM = pl.BlockSpec(memory_space=pltpu.HBM)
PARAMS = pltpu.CompilerParams(vmem_limit_bytes=16 * 1024 * 1024)


def place():
    return lax.axis_index("groups"), lax.axis_index("dp"), lax.axis_index("mp")


def piece(index, size):
    return pl.ds(pl.multiple_of(index * size, size), size)


def prepare_kernel(
    leaving, counts, upstream, tenants, up, down, hidden, weighted, my_cols, sooner, later, block,
    held_counts, held_upstream, held_tenants, held_up, held_down, held_hidden, sem,
):
    _, _, m = place()
    _, own_blocks, part_rank, _ = block.shape
    loads = [
        pltpu.make_async_copy(source, target, sem.at[i])
        for i, (source, target) in enumerate(
            [
                (counts, held_counts),
                (upstream, held_upstream),
                (tenants, held_tenants),
                (up, held_up),
                (down.at[piece(m, part_rank)], held_down),
                (hidden, held_hidden),
            ]
        )
    ]
    for load in loads[:2] + loads[5:] + loads[2:5]:
        load.start()
    rows, part = my_cols.shape
    diagonal = lax.broadcasted_iota(jnp.int32, (rows, rows), 0) == lax.broadcasted_iota(jnp.int32, (rows, rows), 1)
    loads[0].wait()
    scale = jnp.where(diagonal, held_counts[...].astype(f32), 0.0).astype(bf16)
    loads[1].wait()
    weighted[...] = jnp.dot(scale, held_upstream[...], preferred_element_type=f32).astype(bf16)
    my_cols[...] = weighted[:, piece(m, part)]
    loads[2].wait()
    loads[3].wait()
    for ks, picked in zip(leaving, (sooner, later)):
        for i, k in enumerate(ks):
            for n in range(own_blocks):
                picked[i, n] = chosen(held_tenants, held_up, k, n, own_blocks, part_rank)
    loads[4].wait()
    loads[5].wait()
    low = lax.dot_general(
        held_down[...], held_hidden[...], (((1,), (1,)), ((), ())), preferred_element_type=f32
    ).astype(bf16)
    size = rows // own_blocks
    for n in range(own_blocks):
        at = slice(n * size, (n + 1) * size)
        block[0, n] = jnp.dot(low[:, at], weighted[at], preferred_element_type=f32).astype(bf16)


def spread_kernel(weight, _, to_send, held, in_sem, out_sem):
    g, _, _ = place()
    copies, depth = to_send.shape[0], to_send.shape[1]
    chunks = in_sem.shape[0]
    size = depth // chunks
    loads, stores = [], []
    for c in range(chunks):
        at = pl.ds(pl.multiple_of(g * depth + c * size, size), size)
        loads.append(pltpu.make_async_copy(weight.at[at], held.at[pl.ds(c * size, size)], in_sem.at[c]))
        loads[-1].start()
    for c in range(chunks):
        loads[c].wait()
        for k in range(copies):
            at = pl.ds(c * size, size)
            stores.append(pltpu.make_async_copy(held.at[at], to_send.at[k, at], out_sem.at[k, c]))
            stores[-1].start()
    for store in stores:
        store.wait()


def chosen(tenants, up, distance, n, own_blocks, part_rank):
    _, d, m = place()
    wanted = tenants[(d ^ distance) * own_blocks + n] - d * up.shape[0]
    total = jnp.zeros((part_rank, up.shape[2]), bf16)
    for t in range(up.shape[0]):
        total = jnp.where(wanted == t, up[t, piece(m, part_rank)], total)
    return total


def pick_kernel(leaving, held, tenants, up, *refs):
    out = refs[-1]
    for i, k in enumerate(leaving):
        for n in range(out.shape[1]):
            value = chosen(tenants, up, k, n, out.shape[1], out.shape[2])
            for kept, got in zip(held, refs[:-1]):
                if k in kept:
                    value = value + got[kept.index(k), n]
            out[i, n] = value


def both_kernel(leaving, held, tenants, up, *refs):
    out = refs[-1]
    pick_kernel(leaving, held, tenants, up, *refs[: len(held)], out.at[: len(leaving)])
    at = len(leaving)
    for blocks in refs[len(held) : -1]:
        out[at : at + blocks.shape[0]] = blocks[...]
        at += blocks.shape[0]


def back_kernel(held, tenants, up, weighted, *refs):
    out = refs[-1]
    part_rank, rows = out.shape
    own_blocks = refs[0].shape[1]
    size = rows // own_blocks
    for n in range(own_blocks):
        value = chosen(tenants, up, 0, n, own_blocks, part_rank)
        for kept, got in zip(held, refs[:-1]):
            if 0 in kept:
                value = value + got[kept.index(0), n]
        at = slice(n * size, (n + 1) * size)
        out[:, at] = lax.dot_general(
            value, weighted[at], (((1,), (1,)), ((), ())), preferred_element_type=f32
        ).astype(bf16)


def gradient_kernel(orders, scale, tenants, *refs):
    out = refs[-1]
    _, d, _ = place()
    for t in range(out.shape[0]):
        total = jnp.zeros(out.shape[1:], f32)
        for order, got in zip(orders, refs[:-1]):
            own_blocks = got.shape[1]
            for i, k in enumerate(order):
                for n in range(own_blocks if k is not None else 0):
                    wanted = tenants[(d ^ k) * own_blocks + n] - d * out.shape[0]
                    total = total + jnp.where(wanted == t, got[i, n].astype(f32), 0.0)
        out[t] = (total * scale).astype(bf16)


def frozen_kernel(near, distances, mine, other, slices, out, held, ready, sem):
    team, rows, part = mine.shape
    count, features, width = slices.shape
    per_part = count // 2
    g, d, m = place()
    own = g * near + lax.rem(d, near)
    for half in range(2):
        at = lax.rem(m + half, 2) * per_part
        for j in range(per_part):
            held[half, :, j * width : (j + 1) * width] = slices[at + j]
    dims = (((1,), (1,)), ((), ()))
    stores = []
    for c in range(0, team, 4):
        total = lax.dot_general(mine[c : c + 4].reshape(4 * rows, part), held[0], dims, preferred_element_type=f32)
        total += lax.dot_general(other[c : c + 4].reshape(4 * rows, part), held[1], dims, preferred_element_type=f32)
        ready[c : c + 4] = total.astype(bf16).reshape(4, rows, features)
        for k in range(c, c + 4):
            stores.append(pltpu.make_async_copy(ready.at[k], out.at[own ^ distances[k]], sem.at[k]))
            stores[-1].start()
    for store in stores:
        store.wait()


def last_kernel(frozen, mine, other, down, gradient, other_gradient, out, whole, back, held, sem, gradient_sem):
    team, rows, features = frozen.shape
    part_rank, _ = mine.shape
    _, _, m = place()
    stores = [
        pltpu.make_async_copy(gradient, whole.at[:, piece(m, part_rank)], gradient_sem.at[0]),
        pltpu.make_async_copy(other_gradient, whole.at[:, piece(1 - m, part_rank)], gradient_sem.at[1]),
    ]
    for store in stores:
        store.start()
    back[piece(m, part_rank)] = mine[...]
    back[piece(1 - m, part_rank)] = other[...]
    for k in range(team):
        at = pl.ds(pl.multiple_of(m * (team * features) + k * features, features), features)
        adapter = lax.dot_general(back[...], down[:, at], (((0,), (0,)), ((), ())), preferred_element_type=f32)
        held[k] = (frozen[k].astype(f32) + adapter_scale * adapter).astype(bf16)
        stores.append(pltpu.make_async_copy(held.at[k], out.at[:, pl.ds(k * features, features)], sem.at[k]))
        stores[-1].start()
    for store in stores:
        store.wait()


def local(
    hidden_input,
    upstream,
    rollout_row_counts,
    tenant_of_block,
    frozen_value_weight,
    common_down_factor,
    adapter_up_factor,
):
    group_count = lax.axis_size("groups")
    dp_count = lax.axis_size("dp")
    mp_count = lax.axis_size("mp")
    half_width, cols = frozen_value_weight.shape
    tenants_here, rank, out_width = adapter_up_factor.shape
    part_rank = rank // mp_count
    part_cols = out_width // mp_count
    rows = hidden_input.shape[0]
    own_blocks = tenant_of_block.shape[0] // dp_count
    block_rows = rows // own_blocks

    near = math.gcd(4, dp_count)
    team = group_count * near
    features = half_width // team
    teams = [
        [(gi * dp_count + base + k) * mp_count + mi for gi in range(group_count) for k in range(near)]
        for base in range(0, dp_count, near)
        for mi in range(mp_count)
    ]

    def swap(value, axis, bit):
        size = lax.axis_size(axis)
        return lax.ppermute(value, axis, [(k, k ^ bit) for k in range(size)])

    def shape(*dims):
        return jax.ShapeDtypeStruct(dims, bf16)

    def call(kernel, name, outs, in_specs, *values, scratch=(), out_specs=VMEM, params=PARAMS):
        return pl.pallas_call(
            kernel, in_specs=in_specs, out_specs=out_specs, out_shape=outs, scratch_shapes=list(scratch),
            compiler_params=params, name=name,
        )(*values)

    dp_bits = [1 << k for k in range(dp_count.bit_length() - 1)]
    near_bits = [bit for bit in dp_bits if bit < near]
    tie = lax.optimization_barrier

    repeats = dp_count // near
    leaving = [[k for k in range(dp_count) if k & 1 and bool(k & 2) == sooner] for sooner in (True, False)]
    remaining = [k for k in range(dp_count) if not k & 1]
    weighted, my_cols, *picked, block = call(
        functools.partial(prepare_kernel, leaving), "prepare",
        [
            shape(rows, out_width),
            shape(rows, part_cols),
            shape(len(leaving[0]), own_blocks, part_rank, out_width),
            shape(len(leaving[1]), own_blocks, part_rank, out_width),
            shape(1, own_blocks, part_rank, out_width),
        ],
        [HBM] * 6, rollout_row_counts[None], upstream, tenant_of_block, adapter_up_factor, common_down_factor.T,
        hidden_input, out_specs=[VMEM] * 5, params=pltpu.CompilerParams(),
        scratch=[
            pltpu.VMEM((1, rows), jnp.int32),
            pltpu.VMEM((rows, out_width), bf16),
            pltpu.SMEM(tenant_of_block.shape, jnp.int32),
            pltpu.VMEM(adapter_up_factor.shape, bf16),
            pltpu.VMEM((part_rank, common_down_factor.shape[0]), bf16),
            pltpu.VMEM(hidden_input.shape, bf16),
            pltpu.SemaphoreType.DMA((6,)),
        ],
    )
    to_send = call(
        spread_kernel, "spread", shape(repeats, near * features, cols), [HBM] * 2, frozen_value_weight, block,
        out_specs=HBM, params=pltpu.CompilerParams(),
        scratch=[
            pltpu.VMEM((near * features, cols), bf16),
            pltpu.SemaphoreType.DMA((4,)),
            pltpu.SemaphoreType.DMA((repeats, 4)),
        ],
    )
    row_steps = [("dp", bit, bit) for bit in near_bits[1:] + near_bits[:1]] + [
        ("groups", 1 << k, near << k) for k in range(group_count.bit_length() - 1)
    ]
    team_rows, distances = my_cols[None], [0]
    held = [[k ^ 1 for k in ks] for ks in leaving]
    got = [swap(value, "dp", 1) for value in picked]

    def useful(keys):
        return [i for i, kept in enumerate(held) if set(kept) & set(keys)]
    pieces, orders = [block], [[0]]
    last = []

    def up_step(bit):
        leaving = [k for k in remaining if k & bit]
        some = useful(leaving)
        value = call(
            functools.partial(pick_kernel, leaving, [held[i] for i in some]), "pick",
            shape(len(leaving), own_blocks, part_rank, out_width), [SMEM, VMEM] + [VMEM] * len(some),
            tenant_of_block, adapter_up_factor, *[got[i] for i in some],
        )
        last.append(value)
        remaining[:] = [k for k in remaining if not k & bit]
        held.append(list(remaining))
        got.append(swap(value, "dp", bit))

    def gathered():
        return [k for order in orders for k in order if k is not None]

    def block_step(bit):
        kept = [value[order.count(None) :] for value, order in zip(pieces, orders)]
        value = jnp.concatenate(kept) if len(kept) > 1 else kept[0]
        last.append(value)
        orders.append([k | bit for k in gathered()])
        pieces.append(swap(value, "dp", bit))

    def both_step(bit):
        leaving = [k for k in remaining if k & bit]
        blocks = gathered()
        some = useful(leaving)
        value = call(
            functools.partial(both_kernel, leaving, [held[i] for i in some]), "both",
            shape(len(leaving) + len(blocks), own_blocks, part_rank, out_width),
            [SMEM, VMEM] + [VMEM] * (len(some) + len(pieces)),
            tenant_of_block, adapter_up_factor, *[got[i] for i in some], *pieces,
        )
        last.append(value)
        remaining[:] = [k for k in remaining if not k & bit]
        arrived = swap(value, "dp", bit)
        held.append(list(remaining))
        got.append(arrived)
        orders.append([None] * len(leaving) + [k | bit for k in blocks])
        pieces.append(arrived)

    up_bits, block_bits = dp_bits[1:], dp_bits[::-1]
    for step, (axis, bit, distance) in enumerate(row_steps):
        new_rows = swap(team_rows, axis, bit)
        if step == 1 and up_bits[0] == block_bits[0]:
            both_step(up_bits.pop(0))
            block_bits.pop(0)
        else:
            if step:
                up_step(up_bits.pop(0))
            block_step(block_bits.pop(0))
        if step == 1:
            to_send, *_ = tie((to_send, team_rows, *last))
        if step == 0:
            team_rows, new_rows, got[:1], to_send = tie((team_rows, new_rows, got[:1], to_send))
        elif step < len(row_steps) - 1:
            team_rows, new_rows, *_ = tie((team_rows, new_rows, got[::2], pieces))
        else:
            new_rows, _ = tie((new_rows, got[1]))
        team_rows = jnp.concatenate([team_rows, new_rows])
        distances = distances + [k | distance for k in distances]
    other_rows = swap(team_rows, "mp", 1)
    weight_slices = lax.all_to_all(
        to_send.reshape(dp_count, features, cols), "dp", split_axis=0, concat_axis=0, tiled=True
    )

    weight_slices, _ = tie((weight_slices, last))
    if cols % 128:
        slices = weight_slices.transpose(1, 0, 2).reshape(features, 2, part_cols).transpose(1, 0, 2)
    else:
        slices = weight_slices
    frozen = call(
        functools.partial(frozen_kernel, near, distances), "frozen", shape(team, rows, features), [VMEM, VMEM, VMEM],
        team_rows, other_rows, slices, out_specs=HBM,
        scratch=[
            pltpu.VMEM((2, features, part_cols), bf16),
            pltpu.VMEM((team, rows, features), bf16),
            pltpu.SemaphoreType.DMA((team,)),
        ],
    )
    frozen, *_ = tie((frozen, got, pieces))
    frozen_mine = lax.all_to_all(
        frozen, ALL, split_axis=0, concat_axis=0, tiled=True, axis_index_groups=teams
    )
    for bit in up_bits:
        up_step(bit)
    for bit in block_bits:
        block_step(bit)
    some = useful([0])
    back_part = call(
        functools.partial(back_kernel, [held[i] for i in some]), "back", shape(part_rank, rows),
        [SMEM, VMEM, VMEM] + [VMEM] * len(some), tenant_of_block, adapter_up_factor, weighted, *[got[i] for i in some],
    )

    grad_part = call(
        functools.partial(gradient_kernel, orders, adapter_scale / block_rows), "gradient",
        shape(tenants_here, part_rank, out_width), [SMEM] + [VMEM] * len(pieces), tenant_of_block, *pieces,
    )
    input_gradient, up_factor_gradient = call(
        last_kernel, "last", [shape(rows, half_width), shape(*adapter_up_factor.shape)], [VMEM] * 6,
        frozen_mine, back_part, swap(back_part, "mp", 1), common_down_factor.T, grad_part, swap(grad_part, "mp", 1),
        out_specs=[HBM, HBM],
        scratch=[
            pltpu.VMEM((rank, rows), bf16),
            pltpu.VMEM((team, rows, features), bf16),
            pltpu.SemaphoreType.DMA((team,)),
            pltpu.SemaphoreType.DMA((2,)),
        ],
    )
    return (input_gradient, up_factor_gradient)


def solution(mesh):
    placed = (
        P(("groups", "dp"), None),
        P(("groups", "dp"), None),
        P(("groups", "dp")),
        P("groups"),
        P("mp", "dp"),
        P(),
        P(("groups", "dp"), None, None),
    )
    return jax.shard_map(
        local,
        mesh=mesh,
        in_specs=placed,
        out_specs=(P(("groups", "dp"), "mp"), P(("groups", "dp"), None, None)),
        check_vma=False,
    )
```
